32 devices in a mesh: tm: 8 (over z, y), det: 4 (over x, core).
Axes of the slice: x: 2, y: 2, z: 4, core: 2. Of those that a mesh axis runs over, the one named last changes fastest.
Arguments:
- solution: float32 [3, 12288, 128], P(None, ('tm', 'det')), may hold values from -30 to 30
- residual: float32 [3, 12288, 128], P(None, ('tm', 'det')), may hold values from -30 to 30
- direction: float32 [3, 12288, 128], P(None, ('tm', 'det')), may hold values from -30 to 30
- preconditioner: float32 [6, 12288, 128], P(None, ('tm', 'det')), may hold values from -3 to 10, as said below
- pull_index: int32 [8, 4, 2, 4, 16], P('tm', 'det'), may hold values from 0 to 383, as said below
- block_slot: int32 [256, 512], P('det', 'tm'), may hold values from 0 to 127, as said below
- pixel_offset: int32 [256, 65536], P('det', 'tm'), may hold values from 0 to 127
- angle_index: int32 [256, 65536], P('det', 'tm'), may hold values from 0 to 63
- det_weight: float32 [256], replicated, may hold values from 1 to 10
- mode_templates: float32 [256, 16], replicated, may hold values from -6 to 6
- mode_precision: float32 [16], replicated, may hold values from 256 to 2560
Outputs:
- new_solution: float32 [3, 12288, 128], P(None, ('tm', 'det'))
- new_residual: float32 [3, 12288, 128], P(None, ('tm', 'det'))
- new_direction: float32 [3, 12288, 128], P(None, ('tm', 'det'))
The draws below stay inside these ranges and needn't reach their ends.
Inputs may be any that keep to these rules, and one draw needn't show every extreme that they name: `preconditioner`: at every pixel the six entries form a symmetric positive definite matrix; the three diagonal entries lie in 1 to 10. `pull_index`: for each owner device, reach and det index the 16 block numbers are distinct. `block_slot`: each aligned run of 4 sample blocks of a detector points into one slot.
All inputs are finite; a program needn't handle non-finite values.
Results may differ from the reference program's by a relative error of at most 0.0003.
Values sent between devices are 32-bit elements; how exact they have to be, the bound alone decides.
No kernel may reach another device: no remote copies, remote signals or barrier semaphores. Data moves between devices by JAX's collectives and lax.ppermute only.
A program may use at most 64 MiB of HBM per device.

```python
import math
import jax
import jax.numpy as jnp
from jax import lax

DET_DEV = 64
SAMP_DEV = 8192
PB = 128
SB = 128
BLK_DEV = 384
REACH = 2
CAP = 16
RUN = 4
MODES = 16
NANG = 64
DETS = 256
SAMPLES = 65536
BLOCKS = 12288
SLOTS = 128
N_TM = 8
N_DET = 4


def shaped_map(key, values):
    trend_line = 1.0 + 2.0 * jnp.arange(BLOCKS, dtype=jnp.float32) / max(BLOCKS - 1, 1)
    roughness = jnp.exp(jax.random.uniform(key, (3, BLOCKS, PB), jnp.float32, -0.7, 0.7))
    return jnp.clip(values * roughness * trend_line[None, :, None], -30.0, 30.0)


def draw_solution(key, part):
    key = jax.random.fold_in(key, 1)
    inner = jax.random.fold_in(key, 7)
    values = jax.random.normal(inner, (3, BLOCKS, PB), jnp.float32)
    return shaped_map(jax.random.fold_in(key, 9), values)


def draw_residual(key, part):
    key = jax.random.fold_in(key, 3)
    inner = jax.random.fold_in(key, 7)
    values = jax.random.normal(inner, (3, BLOCKS, PB), jnp.float32)
    return shaped_map(jax.random.fold_in(key, 9), values)


def draw_direction(key, part):
    key = jax.random.fold_in(key, 5)
    inner = jax.random.fold_in(key, 7)
    values = jax.random.normal(inner, (3, BLOCKS, PB), jnp.float32)
    return shaped_map(jax.random.fold_in(key, 9), values)


def draw_preconditioner(key, part):
    key = jax.random.fold_in(key, 11)
    diagonal = jnp.exp(jax.random.uniform(jax.random.fold_in(key, 1), (3, BLOCKS, PB), jnp.float32, 0.0, math.log(10.0)))
    coupling = jax.random.uniform(jax.random.fold_in(key, 2), (3, BLOCKS, PB), jnp.float32, -0.3, 0.3)
    first_pair = coupling[0] * jnp.sqrt(diagonal[0] * diagonal[1])
    second_pair = coupling[1] * jnp.sqrt(diagonal[0] * diagonal[2])
    third_pair = coupling[2] * jnp.sqrt(diagonal[1] * diagonal[2])
    return jnp.concatenate([diagonal, jnp.stack([first_pair, second_pair, third_pair])], axis=0)


def draw_pull_index(key, part):
    key = jax.random.fold_in(key, 13)
    scores = jax.random.randint(key, (N_TM, N_DET, REACH, N_DET, BLK_DEV), 0, 1 << 20)
    scores = scores * BLK_DEV + jnp.arange(BLK_DEV, dtype=jnp.int32)
    ranked = jnp.argsort(scores, axis=-1)
    return ranked[..., :CAP].astype(jnp.int32)


def draw_block_slot(key, part):
    key = jax.random.fold_in(key, 17)
    runs = jax.random.randint(key, (DETS, SAMPLES // SB // RUN), 0, SLOTS)
    runs = runs.at[0, 0].set(SLOTS - 1).at[0, 1].set(0)
    return jnp.repeat(runs, RUN, axis=1).astype(jnp.int32)


def place_ends(drawn, key, least, largest):
    extent = drawn.shape
    index_at = [jax.random.randint(jax.random.fold_in(key, axis), (), 0, extent[axis]) for axis in range(len(extent))]
    drawn = drawn.at[tuple(index_at)].set(least)
    longest = extent.index(max(extent))
    index_at[longest] = (index_at[longest] + 1) % extent[longest]
    return drawn.at[tuple(index_at)].set(largest)


def normal_values(own_key, dims, width, most, kind=jnp.bfloat16):
    values = jax.random.normal(own_key, dims, jnp.float32) * width
    return jnp.minimum(jnp.maximum(values, -most), most).astype(kind)


def setup_inputs(seed: int = 0) -> dict:
    splits = jax.random.split(jax.random.key(seed), 12)
    return {
        "solution": draw_solution(jax.random.fold_in(splits[11], 71), 0),
        "residual": draw_residual(jax.random.fold_in(splits[11], 71), 0),
        "direction": draw_direction(jax.random.fold_in(splits[11], 71), 0),
        "preconditioner": draw_preconditioner(jax.random.fold_in(splits[11], 71), 0),
        "pull_index": draw_pull_index(jax.random.fold_in(splits[11], 71), 0),
        "block_slot": draw_block_slot(jax.random.fold_in(splits[11], 71), 0),
        "pixel_offset": place_ends(jax.random.randint(splits[6], (DETS, SAMPLES), 0, PB), jax.random.fold_in(splits[6], 1), 0, PB - 1).astype(jnp.int32),
        "angle_index": place_ends(jax.random.randint(splits[7], (DETS, SAMPLES), 0, NANG), jax.random.fold_in(splits[7], 1), 0, NANG - 1).astype(jnp.int32),
        "det_weight": jnp.clip(jnp.exp(jax.random.uniform(splits[8], (DETS,), jnp.float32, math.log(1.0), math.log(10.0))), 1.0, 10.0),
        "mode_templates": normal_values(splits[9], (DETS, MODES), 1.0, 6.0, jnp.float32),
        "mode_precision": jnp.clip(jnp.exp(jax.random.uniform(splits[10], (MODES,), jnp.float32, math.log(256.0), math.log(2560.0))), 256.0, 2560.0),
    }


def precondition(preconditioner, map_field):
    first = preconditioner[0] * map_field[0] + preconditioner[3] * map_field[1] + preconditioner[4] * map_field[2]
    second = preconditioner[3] * map_field[0] + preconditioner[1] * map_field[1] + preconditioner[5] * map_field[2]
    third = preconditioner[4] * map_field[0] + preconditioner[5] * map_field[1] + preconditioner[2] * map_field[2]
    return jnp.stack([first, second, third])

def reference(solution, residual, direction, preconditioner, pull_index, block_slot, pixel_offset, angle_index, det_weight, mode_templates, mode_precision):
    highest = lax.Precision.HIGHEST
    dets, samples = pixel_offset.shape

    def row_pixels(pieces):
        slot_row, offset_row, detector = pieces
        slot_full = jnp.repeat(slot_row, SB)
        reach_ids = slot_full // (N_DET * CAP)
        owner_det = slot_full // CAP % N_DET
        pick_slot = slot_full % CAP
        stretch_ids = jnp.arange(samples, dtype=jnp.int32) // SAMP_DEV
        owner_tm = (stretch_ids + reach_ids) % N_TM
        group_id = detector // DET_DEV
        local_id = pull_index[owner_tm, owner_det, reach_ids, group_id, pick_slot]
        global_block = (owner_tm * N_DET + owner_det) * BLK_DEV + local_id
        return (global_block * PB + offset_row).astype(jnp.int32)
    pixel_ids = lax.map(row_pixels, (block_slot, pixel_offset, jnp.arange(dets, dtype=jnp.int32)))
    angle_rad = angle_index.astype(jnp.float32) * (2.0 * math.pi / NANG)
    cos_vals = jnp.cos(angle_rad)
    sin_vals = jnp.sin(angle_rad)
    flat_dir = direction.reshape(3, -1)
    timeline = flat_dir[0][pixel_ids] + cos_vals * flat_dir[1][pixel_ids] + sin_vals * flat_dir[2][pixel_ids]
    core_matrix = jnp.diag(mode_precision) + jnp.dot(mode_templates.T, det_weight[:, None] * mode_templates, precision=highest)
    factor = jnp.linalg.cholesky(core_matrix)
    projection = jnp.dot(mode_templates.T, det_weight[:, None] * timeline, precision=highest)
    mode_coef = jax.scipy.linalg.cho_solve((factor, True), projection)
    filtered = det_weight[:, None] * (timeline - jnp.dot(mode_templates, mode_coef, precision=highest))
    spread = jnp.stack([filtered, cos_vals * filtered, sin_vals * filtered]).reshape(3, -1)
    operated = jnp.zeros((3, BLOCKS * PB), jnp.float32).at[:, pixel_ids.reshape(-1)].add(spread)
    operated = operated.reshape(3, BLOCKS, PB)
    rz_old = jnp.sum(residual * precondition(preconditioner, residual))
    curv_sum = jnp.sum(direction * operated)
    step_size = rz_old / curv_sum
    new_solution = solution + step_size * direction
    new_residual = residual - step_size * operated
    applied = precondition(preconditioner, new_residual)
    rz_new = jnp.sum(new_residual * applied)
    new_direction = applied + rz_new / rz_old * direction
    return (new_solution, new_residual, new_direction)
```

```python
import functools
import math

import jax
import jax.numpy as jnp
from jax import lax
from jax.experimental import pallas as pl
from jax.experimental.pallas import tpu as pltpu
from jax.sharding import PartitionSpec as P

PB = 128
SB = 128
RUN = 4
NANG = 64
GROUP = 8
RUN_LEN = RUN * SB
ROWS = 8
LOW = 32
HIGH = PB // LOW
F32 = jnp.float32
BF16 = jnp.bfloat16
HIGHEST = lax.Precision.HIGHEST
VMEM_LIMIT = 48 * 1024 * 1024


def vmem_spec():
    return pl.BlockSpec(memory_space=pltpu.VMEM)


def smem_spec():
    return pl.BlockSpec(memory_space=pltpu.SMEM)


def params():
    return pltpu.CompilerParams(vmem_limit_bytes=VMEM_LIMIT)


def lane_pick(table, index):
    return jnp.take_along_axis(table, index, axis=1, mode="promise_in_bounds")


def wide_pick(table, index):
    parts = [
        lane_pick(table, index[:, PB * part : PB * (part + 1)])
        for part in range(index.shape[1] // PB)
    ]
    return jnp.concatenate(parts, axis=1)


def precondition(pre, field):
    return (
        pre[0] * field[0] + pre[3] * field[1] + pre[4] * field[2],
        pre[3] * field[0] + pre[1] * field[1] + pre[5] * field[2],
        pre[4] * field[0] + pre[5] * field[1] + pre[2] * field[2],
    )


def pull_kernel(request_ref, direction_ref, piece_ref):
    reach_count, group_count, cap_count = request_ref.shape
    for reach in range(reach_count):
        for group in range(group_count):
            for slot in range(cap_count):
                block = request_ref[reach, group, slot]
                for k in range(3):
                    piece_ref[reach, group, pl.ds(k * cap_count + slot, 1), :] = direction_ref[
                        k, pl.ds(block, 1), :
                    ]


def pull_blocks(requests, direction):
    reach_count, group_count, cap_count = requests.shape
    return pl.pallas_call(
        pull_kernel,
        out_shape=jax.ShapeDtypeStruct((reach_count, group_count, 3 * cap_count, PB), F32),
        in_specs=[smem_spec(), vmem_spec()],
        out_specs=vmem_spec(),
        compiler_params=params(),
        name="pull_blocks",
    )(requests, direction)


def timeline_kernel(
    slot_ref, near_ref, far_ref, trig_ref, weighted_ref, offset_ref, angle_ref, time_ref, proj_ref, map_ref, table_ref
):
    step = pl.program_id(0)
    cap_count = near_ref.shape[1] // 3
    group_count = near_ref.shape[0]
    det_count, chunk = offset_ref.shape
    runs = chunk // RUN_LEN

    @pl.when(step == 0)
    def _():
        for reach, ref in enumerate((near_ref, far_ref)):
            for group in range(group_count):
                first = (reach * group_count + group) * cap_count * ROWS
                for k in range(3):
                    map_ref[pl.ds(first + k, cap_count, stride=ROWS), :] = ref[
                        group, pl.ds(k * cap_count, cap_count), :
                    ]

    trig = trig_ref[...]

    def body(group, carry):
        first = pl.multiple_of(group * GROUP, GROUP)
        for run in range(runs):
            for det in range(GROUP):
                slot = slot_ref[first + det, (step * runs + run) * RUN]
                table_ref[run, pl.ds(det * ROWS, ROWS), :] = map_ref[
                    pl.ds(pl.multiple_of(slot * ROWS, ROWS), ROWS), :
                ]
            tables = [table_ref[run, pl.ds(k, GROUP, stride=ROWS), :] for k in range(3)]
            for part in range(RUN):
                lanes = pl.ds(run * RUN_LEN + part * SB, SB)
                offset = offset_ref[pl.ds(first, GROUP), lanes]
                angle = angle_ref[pl.ds(first, GROUP), lanes]
                cos_vals = lane_pick(trig, angle)
                sin_vals = lane_pick(trig, angle + NANG)
                time_ref[pl.ds(first, GROUP), lanes] = (
                    lane_pick(tables[0], offset)
                    + cos_vals * lane_pick(tables[1], offset)
                    + sin_vals * lane_pick(tables[2], offset)
                )
        return carry

    lax.fori_loop(0, det_count // GROUP, body, 0, unroll=2)
    proj_ref[...] = jnp.dot(
        weighted_ref[...], time_ref[...], precision=HIGHEST, preferred_element_type=F32
    )


def make_timeline(block_slot, near, far, trig, weighted, pixel_offset, angle_index, chunk):
    det_dev, samp_dev = pixel_offset.shape
    modes = weighted.shape[0]
    slot_total = 2 * near.shape[0] * (near.shape[1] // 3)
    runs = chunk // RUN_LEN
    wide = pl.BlockSpec((det_dev, chunk), lambda i: (0, i))
    return pl.pallas_call(
        timeline_kernel,
        grid=(samp_dev // chunk,),
        out_shape=(
            jax.ShapeDtypeStruct((det_dev, samp_dev), F32),
            jax.ShapeDtypeStruct((modes, samp_dev), F32),
        ),
        in_specs=[smem_spec()] + [vmem_spec()] * 4 + [wide, wide],
        out_specs=(wide, pl.BlockSpec((modes, chunk), lambda i: (0, i))),
        scratch_shapes=[
            pltpu.VMEM((slot_total * ROWS, PB), F32),
            pltpu.VMEM((runs, GROUP * ROWS, PB), F32),
        ],
        compiler_params=params(),
        name="make_timeline",
    )(block_slot, near, far, trig, weighted, pixel_offset, angle_index)


def bin_kernel(
    slot_ref, proj_ref, trig_ref, back_ref, weight_ref, offset_ref, angle_ref, time_ref, piece_ref, map_ref, row_ref, filt_ref
):
    step = pl.program_id(0)
    reach_count, group_count, rows, _ = piece_ref.shape
    cap_count = rows // 3
    det_count, chunk = offset_ref.shape
    runs = chunk // RUN_LEN

    @pl.when(step == 0)
    def _():
        map_ref[...] = jnp.zeros_like(map_ref)
        row_ref[...] = jnp.zeros_like(row_ref)

    common = jnp.dot(back_ref[...], proj_ref[...], precision=HIGHEST, preferred_element_type=F32)
    filt_ref[...] = weight_ref[...] * (time_ref[...] - common)
    trig = trig_ref[...]
    det_iota = lax.broadcasted_iota(jnp.int32, (GROUP, RUN_LEN), 0)
    low_iota = lax.broadcasted_iota(jnp.int32, (LOW, RUN_LEN), 0).astype(F32).astype(BF16)
    row_iota = lax.broadcasted_iota(jnp.int32, (GROUP, PB), 0)
    lane_iota = lax.broadcasted_iota(jnp.int32, (GROUP, PB), 1)
    own_lanes = lane_iota // LOW == row_iota % HIGH
    zero = jnp.zeros((), BF16)
    one = jnp.ones((), BF16)

    def body(group, carry):
        first = pl.multiple_of(group * GROUP, GROUP)
        for run in range(runs):
            lanes = pl.ds(run * RUN_LEN, RUN_LEN)
            offset = offset_ref[pl.ds(first, GROUP), lanes]
            angle = angle_ref[pl.ds(first, GROUP), lanes]
            filtered = filt_ref[pl.ds(first, GROUP), lanes]
            cos_vals = wide_pick(trig, angle)
            sin_vals = wide_pick(trig, angle + NANG)
            packed = []
            for value in (filtered, cos_vals * filtered, sin_vals * filtered):
                upper = value.astype(BF16).astype(F32)
                packed.append(jnp.concatenate([upper, value - upper], axis=0).astype(BF16))
            turn = ((offset // LOW) - det_iota) & (HIGH - 1)
            turn = turn.astype(F32)
            turn = jnp.concatenate([turn, turn], axis=0).astype(BF16)
            left = jnp.concatenate(
                [jnp.where(turn == jnp.asarray(j, BF16), value, zero) for j in range(HIGH) for value in packed],
                axis=0,
            )
            low = (offset & (LOW - 1)).astype(F32)
            hots = []
            for det in range(GROUP):
                line = jnp.broadcast_to(low[det : det + 1, :], (LOW, RUN_LEN)).astype(BF16)
                hots.append(jnp.where(line == low_iota, one, zero))
            right = jnp.concatenate(hots, axis=0)
            product = lax.dot_general(
                left, right, (((1,), (1,)), ((), ())), preferred_element_type=F32
            )
            for k in range(3):
                total = None
                for j in range(HIGH):
                    top = (j * 3 + k) * 2 * GROUP
                    pair = product[top : top + GROUP] + product[top + GROUP : top + 2 * GROUP]
                    part = jnp.where(row_iota < HIGH, pair[:, :PB], pair[:, PB:])
                    part = jnp.where(own_lanes, part, 0.0)
                    if j:
                        part = pltpu.roll(part, LOW * j, 1)
                    total = part if total is None else total + part
                row_ref[run, pl.ds(k, GROUP, stride=ROWS), :] = total
            for det in range(GROUP):
                slot = slot_ref[first + det, (step * runs + run) * RUN]
                at = pl.ds(pl.multiple_of(slot * ROWS, ROWS), ROWS)
                map_ref[at, :] += row_ref[run, pl.ds(det * ROWS, ROWS), :]
        return carry

    lax.fori_loop(0, det_count // GROUP, body, 0, unroll=1)

    @pl.when(step == pl.num_programs(0) - 1)
    def _():
        for reach in range(reach_count):
            for group in range(group_count):
                start = (reach * group_count + group) * cap_count * ROWS
                for k in range(3):
                    piece_ref[reach, group, pl.ds(k * cap_count, cap_count), :] = map_ref[
                        pl.ds(start + k, cap_count, stride=ROWS), :
                    ]


def bin_samples(block_slot, projection, trig, back, weight, pixel_offset, angle_index, timeline, shape, chunk):
    det_dev, samp_dev = pixel_offset.shape
    modes = projection.shape[0]
    reach_count, group_count, cap_count = shape
    slot_total = reach_count * group_count * cap_count
    runs = chunk // RUN_LEN
    wide = pl.BlockSpec((det_dev, chunk), lambda i: (0, i))
    return pl.pallas_call(
        bin_kernel,
        grid=(samp_dev // chunk,),
        out_shape=jax.ShapeDtypeStruct((reach_count, group_count, 3 * cap_count, PB), F32),
        in_specs=[smem_spec(), pl.BlockSpec((modes, chunk), lambda i: (0, i))]
        + [vmem_spec()] * 3
        + [wide, wide, wide],
        out_specs=vmem_spec(),
        scratch_shapes=[
            pltpu.VMEM((slot_total * ROWS, PB), F32),
            pltpu.VMEM((runs, GROUP * ROWS, PB), F32),
            pltpu.VMEM((det_dev, chunk), F32),
        ],
        compiler_params=params(),
        name="bin_samples",
    )(block_slot, projection, trig, back, weight, pixel_offset, angle_index, timeline)


def push_kernel(request_ref, near_ref, far_ref, operated_ref):
    reach_count, group_count, cap_count = request_ref.shape
    operated_ref[...] = jnp.zeros_like(operated_ref)
    for reach, ref in enumerate((near_ref, far_ref)):
        for group in range(group_count):
            sums = []
            for slot in range(cap_count):
                block = request_ref[reach, group, slot]
                for k in range(3):
                    line = operated_ref[k, pl.ds(block, 1), :]
                    sums.append((block, k, line + ref[group, pl.ds(k * cap_count + slot, 1), :]))
            for block, k, line in sums:
                operated_ref[k, pl.ds(block, 1), :] = line


def push_blocks(requests, near, far, shape):
    return pl.pallas_call(
        push_kernel,
        out_shape=jax.ShapeDtypeStruct(shape, F32),
        in_specs=[smem_spec(), vmem_spec(), vmem_spec()],
        out_specs=vmem_spec(),
        compiler_params=params(),
        name="push_blocks",
    )(requests, near, far)


def exchanged(value, axis, bit):
    count = lax.axis_size(axis)
    return lax.ppermute(value, axis, [(source, source ^ bit) for source in range(count)])


def passed_along(value, axis, steps):
    count = lax.axis_size(axis)
    return lax.ppermute(value, axis, [(source, (source + steps) % count) for source in range(count)])


def summed_over_det(value):
    count = lax.axis_size("det")
    modes, samples = value.shape
    half = samples // 2
    core = lax.axis_index("det") % 2
    own = lax.dynamic_slice_in_dim(value, core * half, half, 1)
    other = lax.dynamic_slice_in_dim(value, (1 - core) * half, half, 1)
    own = own + exchanged(other, "det", 1)
    bit = 2
    while bit < count:
        own = own + exchanged(own, "det", bit)
        bit *= 2
    other = exchanged(own, "det", 1)
    lower = jnp.where(core == 0, own, other)
    upper = jnp.where(core == 0, other, own)
    return jnp.concatenate([lower, upper], axis=1)


def on_device(
    solution,
    residual,
    direction,
    preconditioner,
    pull_index,
    block_slot,
    pixel_offset,
    angle_index,
    det_weight,
    mode_templates,
    mode_precision,
):
    requests = pull_index[0, 0]
    det_dev, samp_dev = pixel_offset.shape
    modes = mode_templates.shape[1]
    device_count = lax.axis_size("tm") * lax.axis_size("det")
    chunk = 1024

    pieces = pull_blocks(requests, direction)
    pieces = lax.all_to_all(pieces, "det", split_axis=1, concat_axis=1, tiled=True)
    near = pieces[0]
    far = passed_along(pieces[1], "tm", -1)

    angles = lax.iota(jnp.int32, NANG).astype(F32) * (2.0 * math.pi / NANG)
    trig = jnp.concatenate([jnp.cos(angles), jnp.sin(angles)])
    trig = jnp.broadcast_to(trig[None, :], (GROUP, PB))
    core_matrix = jnp.diag(mode_precision) + jnp.dot(
        mode_templates.T, det_weight[:, None] * mode_templates, precision=HIGHEST
    )
    factor = jnp.linalg.cholesky(core_matrix)
    first_row = lax.axis_index("det") * det_dev
    own_modes = lax.dynamic_slice_in_dim(mode_templates, first_row, det_dev, 0)
    own_weight = lax.dynamic_slice_in_dim(det_weight, first_row, det_dev, 0)
    inverse = jax.scipy.linalg.cho_solve((factor, True), jnp.eye(modes, dtype=F32))
    back = jnp.dot(own_modes, inverse, precision=HIGHEST)
    weighted = (own_weight[:, None] * own_modes).T

    timeline, local_proj = make_timeline(
        block_slot, near, far, trig, weighted, pixel_offset, angle_index, chunk
    )
    projection = summed_over_det(local_proj)
    binned = bin_samples(
        block_slot, projection, trig, back, own_weight[:, None], pixel_offset, angle_index, timeline,
        requests.shape, chunk,
    )
    returning = jnp.stack([binned[0], passed_along(binned[1], "tm", 1)])
    arrived = lax.all_to_all(returning, "det", split_axis=1, concat_axis=1, tiled=True)
    operated = push_blocks(requests, arrived[0], arrived[1], direction.shape)

    old_applied = jnp.stack(precondition(preconditioner, residual))
    operated_applied = jnp.stack(precondition(preconditioner, operated))
    partial = jnp.stack(
        [
            jnp.sum(residual * old_applied),
            jnp.sum(direction * operated),
            jnp.sum(operated * old_applied),
            jnp.sum(operated * operated_applied),
        ]
    )
    sent = jnp.broadcast_to(jnp.pad(partial, (0, PB - 4))[None, :], (device_count, PB))
    totals = jnp.sum(
        lax.all_to_all(sent, ("tm", "det"), split_axis=0, concat_axis=0, tiled=True), axis=0
    )
    rz_old, curv_sum, cross, square = totals[0], totals[1], totals[2], totals[3]
    step_size = rz_old / curv_sum
    rz_new = rz_old - 2.0 * step_size * cross + step_size * step_size * square
    new_solution = solution + step_size * direction
    new_residual = residual - step_size * operated
    applied = jnp.stack(precondition(preconditioner, new_residual))
    new_direction = applied + rz_new / rz_old * direction
    return (new_solution, new_residual, new_direction)


def solution(mesh):
    maps = P(None, ("tm", "det"), None)
    samples = P("det", "tm")
    in_specs = (maps,) * 4 + (P("tm", "det", None, None, None),) + (samples,) * 3 + (P(),) * 3
    return jax.shard_map(
        on_device, mesh=mesh, in_specs=in_specs, out_specs=(maps,) * 3, check_vma=False
    )
```

```python
import math

import jax
import jax.numpy as jnp
import numpy as np
from jax import lax
from jax.experimental import pallas as pl
from jax.experimental.pallas import tpu as pltpu
from jax.sharding import PartitionSpec as P

PB = 128
SB = 128
RUN = 4
NANG = 64
GROUP = 8
RUN_LEN = RUN * SB
ROWS = 8
LOW = 32
HIGH = PB // LOW
F32 = jnp.float32
BF16 = jnp.bfloat16
HIGHEST = lax.Precision.HIGHEST
MIB = 1024 * 1024
TERMS = 8


def vmem_spec():
    return pl.BlockSpec(memory_space=pltpu.VMEM)


def smem_spec():
    return pl.BlockSpec(memory_space=pltpu.SMEM)


def params(mib):
    return pltpu.CompilerParams(vmem_limit_bytes=mib * MIB)


def wave_terms():
    turn = (np.arange(NANG) - NANG // 2).astype(np.float64) / NANG
    powers = np.stack([turn ** (2 * term) for term in range(TERMS)], axis=1)
    even = np.linalg.lstsq(powers, -np.cos(2.0 * math.pi * turn), rcond=None)[0]
    odd = np.linalg.lstsq(powers * turn[:, None], -np.sin(2.0 * math.pi * turn), rcond=None)[0]
    return [float(term) for term in even], [float(term) for term in odd]


EVEN_TERMS, ODD_TERMS = wave_terms()


def waves(angle):
    turn = (angle - NANG // 2).astype(F32) * (1.0 / NANG)
    square = turn * turn
    even = jnp.full_like(turn, EVEN_TERMS[-1])
    odd = jnp.full_like(turn, ODD_TERMS[-1])
    for term in range(TERMS - 2, -1, -1):
        even = even * square + EVEN_TERMS[term]
        odd = odd * square + ODD_TERMS[term]
    return even, odd * turn


def trig_table():
    angles = (np.arange(NANG, dtype=np.float32) * np.float32(2.0 * math.pi / NANG)).astype(np.float64)
    row = np.concatenate([np.cos(angles), np.sin(angles)]).astype(np.float32)
    return jnp.asarray(np.broadcast_to(row[None, :], (GROUP, PB)))


def halves(value):
    first = value.astype(BF16)
    rest = value - first.astype(F32)
    second = rest.astype(BF16)
    return first, second, (rest - second.astype(F32)).astype(BF16)


def lane_pick(table, index):
    return jnp.take_along_axis(table, index, axis=1, mode="promise_in_bounds")


def wide_pick(table, index):
    parts = [
        lane_pick(table, index[:, PB * part : PB * (part + 1)])
        for part in range(index.shape[1] // PB)
    ]
    return jnp.concatenate(parts, axis=1)


def precondition(pre, field):
    return (
        pre[0] * field[0] + pre[3] * field[1] + pre[4] * field[2],
        pre[3] * field[0] + pre[1] * field[1] + pre[5] * field[2],
        pre[4] * field[0] + pre[5] * field[1] + pre[2] * field[2],
    )


def partner(det, hop, flip):
    return det ^ (2 * hop + flip)


def pull_kernel(det_ref, request_ref, direction_ref, own_ref, other_ref):
    _, _, reach_count, group_count, cap_count = request_ref.shape
    det = det_ref[0]
    for flip, ref in ((1, other_ref), (0, own_ref)):
        for reach in range(reach_count):
            for hop in range(group_count // 2):
                group = partner(det, hop, flip)
                for slot in range(cap_count):
                    block = request_ref[0, 0, reach, group, slot]
                    for k in range(3):
                        ref[reach, hop, pl.ds(k * cap_count + slot, 1), :] = direction_ref[
                            k, pl.ds(block, 1), :
                        ]


def pull_blocks(det, pull_index, direction):
    _, _, reach_count, group_count, cap_count = pull_index.shape
    piece = jax.ShapeDtypeStruct((reach_count, group_count // 2, 3 * cap_count, PB), F32)
    return pl.pallas_call(
        pull_kernel,
        out_shape=(piece, piece),
        in_specs=[smem_spec(), smem_spec(), vmem_spec()],
        out_specs=(vmem_spec(), vmem_spec()),
        compiler_params=params(8),
        name="pull_blocks",
    )(det, pull_index, direction)


def mode_kernel(det_ref, template_ref, weight_ref, precision_ref, back_ref, weighted_ref, own_weight_ref):
    det_dev = back_ref.shape[0]
    modes = template_ref.shape[1]
    templates = template_ref[...]
    weight = weight_ref[...]
    first = pl.multiple_of(det_ref[0] * det_dev, det_dev)
    own_templates = template_ref[pl.ds(first, det_dev), :]
    own_weight = weight_ref[pl.ds(first, det_dev), :]
    own_weight_ref[...] = own_weight
    weighted_ref[...] = (own_templates * own_weight).T
    row = lax.broadcasted_iota(jnp.int32, (modes, modes), 0)
    column = lax.broadcasted_iota(jnp.int32, (modes, modes), 1)
    unit = (row == column).astype(F32)
    core = unit * precision_ref[...] + lax.dot_general(
        weight * templates, templates, (((0,), (0,)), ((), ())), precision=HIGHEST, preferred_element_type=F32
    )
    inverse = unit
    line = lax.broadcasted_iota(jnp.int32, (modes, 1), 0)
    for step in range(modes):
        root = 1.0 / jnp.sqrt(core[step : step + 1, step : step + 1])
        factor = jnp.where(line > step, core[:, step : step + 1] * root, 0.0)
        core_row = core[step : step + 1, :] * root
        inverse_row = inverse[step : step + 1, :] * root
        core = core - factor * core_row
        inverse = jnp.where(line == step, inverse_row, inverse - factor * inverse_row)
    solved = lax.dot_general(
        inverse, inverse, (((0,), (0,)), ((), ())), precision=HIGHEST, preferred_element_type=F32
    )
    back_ref[...] = jnp.dot(own_templates, solved, precision=HIGHEST, preferred_element_type=F32)


def mode_matrices(det, det_dev, mode_templates, det_weight, mode_precision):
    modes = mode_templates.shape[1]
    return pl.pallas_call(
        mode_kernel,
        out_shape=(
            jax.ShapeDtypeStruct((det_dev, modes), F32),
            jax.ShapeDtypeStruct((modes, det_dev), F32),
            jax.ShapeDtypeStruct((det_dev, 1), F32),
        ),
        in_specs=[smem_spec(), vmem_spec(), vmem_spec(), vmem_spec()],
        out_specs=(vmem_spec(), vmem_spec(), vmem_spec()),
        compiler_params=params(8),
        name="mode_matrices",
    )(det, mode_templates, det_weight[:, None], mode_precision[None, :])


def timeline_kernel(det_ref, slot_ref, weighted_ref, offset_ref, angle_ref, *refs):
    *piece_refs, time_ref, proj_ref, map_ref, table_ref = refs
    step = pl.program_id(0)
    cap_count = piece_refs[0].shape[1] // 3
    hop_count = len(piece_refs) // 2
    det_count, chunk = offset_ref.shape
    runs = chunk // RUN_LEN

    @pl.when(step == 0)
    def _():
        det = det_ref[0]
        for place, ref in enumerate(piece_refs):
            reach, hop = place // hop_count, place % hop_count
            for flip in range(2):
                block = (reach * 2 * hop_count + partner(det, hop, flip)) * cap_count
                first = pl.multiple_of(block * ROWS, cap_count * ROWS)
                for k in range(3):
                    map_ref[pl.ds(first + k, cap_count, stride=ROWS), :] = ref[
                        flip, pl.ds(k * cap_count, cap_count), :
                    ]

    def body(group, carry):
        first = pl.multiple_of(group * GROUP, GROUP)
        for run in range(runs):
            for det in range(GROUP):
                slot = slot_ref[first + det, (step * runs + run) * RUN]
                table_ref[run, pl.ds(det * ROWS, ROWS), :] = map_ref[
                    pl.ds(pl.multiple_of(slot * ROWS, ROWS), ROWS), :
                ]
            tables = [table_ref[run, pl.ds(k, GROUP, stride=ROWS), :] for k in range(3)]
            for part in range(RUN):
                lanes = pl.ds(run * RUN_LEN + part * SB, SB)
                offset = offset_ref[pl.ds(first, GROUP), lanes]
                angle = angle_ref[pl.ds(first, GROUP), lanes]
                cos_vals, sin_vals = waves(angle)
                time_ref[pl.ds(first, GROUP), lanes] = (
                    lane_pick(tables[0], offset)
                    + cos_vals * lane_pick(tables[1], offset)
                    + sin_vals * lane_pick(tables[2], offset)
                )
        return carry

    lax.fori_loop(0, det_count // GROUP, body, 0, unroll=4)
    proj_ref[...] = jnp.dot(
        weighted_ref[...], time_ref[...], precision=HIGHEST, preferred_element_type=F32
    )


def make_timeline(det, block_slot, weighted, pixel_offset, angle_index, pieces, chunk):
    det_dev, samp_dev = pixel_offset.shape
    modes = weighted.shape[0]
    slot_total = len(pieces) * 2 * (pieces[0].shape[1] // 3)
    runs = chunk // RUN_LEN
    wide = pl.BlockSpec((det_dev, chunk), lambda i: (0, i))
    return pl.pallas_call(
        timeline_kernel,
        grid=(samp_dev // chunk,),
        out_shape=(
            jax.ShapeDtypeStruct((det_dev, samp_dev), F32),
            jax.ShapeDtypeStruct((modes, samp_dev), F32),
        ),
        in_specs=[smem_spec(), smem_spec(), vmem_spec(), wide, wide] + [vmem_spec()] * len(pieces),
        out_specs=(wide, pl.BlockSpec((modes, chunk), lambda i: (0, i))),
        scratch_shapes=[
            pltpu.VMEM((slot_total * ROWS, PB), F32),
            pltpu.VMEM((runs, GROUP * ROWS, PB), F32),
        ],
        compiler_params=params(16),
        name="make_timeline",
    )(det, block_slot, weighted, pixel_offset, angle_index, *pieces)


def bin_kernel(
    det_ref, slot_ref, proj_ref, trig_ref, back_ref, weight_ref, offset_ref, angle_ref, time_ref,
    own_ref, other_ref, map_ref, row_ref, filt_ref,
):
    step = pl.program_id(0)
    reach_count, hop_count, rows, _ = own_ref.shape
    cap_count = rows // 3
    det_count, chunk = offset_ref.shape
    runs = chunk // RUN_LEN

    @pl.when(step == 0)
    def _():
        map_ref[...] = jnp.zeros_like(map_ref)
        row_ref[...] = jnp.zeros_like(row_ref)

    back = halves(back_ref[...])
    proj = halves(proj_ref[...])
    orders = ((0, 0), (0, 1), (1, 0), (0, 2), (1, 1), (2, 0))
    common = jnp.dot(
        jnp.concatenate([back[left] for left, _ in orders], axis=1),
        jnp.concatenate([proj[right] for _, right in orders], axis=0),
        preferred_element_type=F32,
    )
    filt_ref[...] = weight_ref[...] * (time_ref[...] - common)
    trig = trig_ref[...]
    det_iota = lax.broadcasted_iota(jnp.int32, (GROUP, RUN_LEN), 0)
    low_iota = lax.broadcasted_iota(jnp.int32, (LOW, RUN_LEN), 0).astype(F32).astype(BF16)
    row_iota = lax.broadcasted_iota(jnp.int32, (GROUP, PB), 0)
    lane_iota = lax.broadcasted_iota(jnp.int32, (GROUP, PB), 1)
    own_lanes = lane_iota // LOW == row_iota % HIGH
    zero = jnp.zeros((), BF16)
    one = jnp.ones((), BF16)

    def body(group, carry):
        first = pl.multiple_of(group * GROUP, GROUP)
        for run in range(runs):
            lanes = pl.ds(run * RUN_LEN, RUN_LEN)
            offset = offset_ref[pl.ds(first, GROUP), lanes]
            angle = angle_ref[pl.ds(first, GROUP), lanes]
            filtered = filt_ref[pl.ds(first, GROUP), lanes]
            cos_vals = wide_pick(trig, angle)
            sin_vals = wide_pick(trig, angle + NANG)
            packed = []
            for value in (filtered, cos_vals * filtered, sin_vals * filtered):
                upper = value.astype(BF16).astype(F32)
                packed.append(jnp.concatenate([upper, value - upper], axis=0).astype(BF16))
            turn = ((offset // LOW) - det_iota) & (HIGH - 1)
            turn = turn.astype(F32)
            turn = jnp.concatenate([turn, turn], axis=0).astype(BF16)
            left = jnp.concatenate(
                [jnp.where(turn == jnp.asarray(j, BF16), value, zero) for j in range(HIGH) for value in packed],
                axis=0,
            )
            low = (offset & (LOW - 1)).astype(F32)
            hots = []
            for det in range(GROUP):
                line = jnp.broadcast_to(low[det : det + 1, :], (LOW, RUN_LEN)).astype(BF16)
                hots.append(jnp.where(line == low_iota, one, zero))
            right = jnp.concatenate(hots, axis=0)
            product = lax.dot_general(
                left, right, (((1,), (1,)), ((), ())), preferred_element_type=F32
            )
            for k in range(3):
                total = None
                for j in range(HIGH):
                    top = (j * 3 + k) * 2 * GROUP
                    pair = product[top : top + GROUP] + product[top + GROUP : top + 2 * GROUP]
                    part = jnp.where(row_iota < HIGH, pair[:, :PB], pair[:, PB:])
                    part = jnp.where(own_lanes, part, 0.0)
                    if j:
                        part = pltpu.roll(part, LOW * j, 1)
                    total = part if total is None else total + part
                row_ref[run, pl.ds(k, GROUP, stride=ROWS), :] = total
            for det in range(GROUP):
                slot = slot_ref[first + det, (step * runs + run) * RUN]
                at = pl.ds(pl.multiple_of(slot * ROWS, ROWS), ROWS)
                map_ref[at, :] += row_ref[run, pl.ds(det * ROWS, ROWS), :]
        return carry

    lax.fori_loop(0, det_count // GROUP, body, 0, unroll=8)

    @pl.when(step == pl.num_programs(0) - 1)
    def _():
        det = det_ref[0]
        for flip, ref in ((1, other_ref), (0, own_ref)):
            for reach in range(reach_count):
                for hop in range(hop_count):
                    block = (reach * 2 * hop_count + partner(det, hop, flip)) * cap_count
                    start = pl.multiple_of(block * ROWS, cap_count * ROWS)
                    for k in range(3):
                        ref[reach, hop, pl.ds(k * cap_count, cap_count), :] = map_ref[
                            pl.ds(start + k, cap_count, stride=ROWS), :
                        ]


def bin_samples(
    det, block_slot, projection, trig, back, weight, pixel_offset, angle_index, timeline, shape, chunk
):
    det_dev, samp_dev = pixel_offset.shape
    modes = projection.shape[0]
    reach_count, group_count, cap_count = shape
    slot_total = reach_count * group_count * cap_count
    runs = chunk // RUN_LEN
    wide = pl.BlockSpec((det_dev, chunk), lambda i: (0, i))
    piece = jax.ShapeDtypeStruct((reach_count, group_count // 2, 3 * cap_count, PB), F32)
    return pl.pallas_call(
        bin_kernel,
        grid=(samp_dev // chunk,),
        out_shape=(piece, piece),
        in_specs=[smem_spec(), smem_spec(), pl.BlockSpec((modes, chunk), lambda i: (0, i))]
        + [vmem_spec()] * 3
        + [wide, wide, wide],
        out_specs=(vmem_spec(), vmem_spec()),
        scratch_shapes=[
            pltpu.VMEM((slot_total * ROWS, PB), F32),
            pltpu.VMEM((runs, GROUP * ROWS, PB), F32),
            pltpu.VMEM((det_dev, chunk), F32),
        ],
        compiler_params=params(24),
        name="bin_samples",
    )(det, block_slot, projection, trig, back, weight, pixel_offset, angle_index, timeline)


def push_kernel(det_ref, request_ref, direction_ref, residual_ref, pre_ref, *refs):
    *piece_refs, operated_ref, part_ref = refs
    cap_count = request_ref.shape[4]
    hop_count = len(piece_refs) // 2
    det = det_ref[0]
    operated_ref[...] = jnp.zeros_like(operated_ref)
    for place, ref in enumerate(piece_refs):
        reach, hop = place // hop_count, place % hop_count
        for flip in range(2):
            group = partner(det, hop, flip)
            sums = []
            for slot in range(cap_count):
                block = request_ref[0, 0, reach, group, slot]
                for k in range(3):
                    line = operated_ref[k, pl.ds(block, 1), :]
                    sums.append((block, k, line + ref[flip, pl.ds(k * cap_count + slot, 1), :]))
            for block, k, line in sums:
                operated_ref[k, pl.ds(block, 1), :] = line

    blocks = operated_ref.shape[1]

    def body(index, totals):
        rows = pl.ds(pl.multiple_of(index * ROWS, ROWS), ROWS)
        pre = [pre_ref[entry, rows, :] for entry in range(6)]
        old = [residual_ref[k, rows, :] for k in range(3)]
        oper = [operated_ref[k, rows, :] for k in range(3)]
        line = [direction_ref[k, rows, :] for k in range(3)]
        old_applied = precondition(pre, old)
        oper_applied = precondition(pre, oper)

        def dot(left, right):
            return left[0] * right[0] + left[1] * right[1] + left[2] * right[2]

        parts = (dot(old, old_applied), dot(line, oper), dot(oper, old_applied), dot(oper, oper_applied))
        return tuple(total + part for total, part in zip(totals, parts))

    nothing = jnp.zeros((ROWS, PB), F32)
    totals = lax.fori_loop(0, blocks // ROWS, body, (nothing,) * 4, unroll=4)
    lane = lax.broadcasted_iota(jnp.int32, part_ref.shape, 1)
    row = jnp.zeros(part_ref.shape, F32)
    for place, total in enumerate(totals):
        value = jnp.sum(jnp.sum(total, axis=0, keepdims=True), axis=1, keepdims=True)
        row = jnp.where(lane == place, value, row)
    part_ref[...] = row


def push_blocks(det, pull_index, direction, residual, preconditioner, pieces, device_count):
    return pl.pallas_call(
        push_kernel,
        out_shape=(
            jax.ShapeDtypeStruct(direction.shape, F32),
            jax.ShapeDtypeStruct((device_count, PB), F32),
        ),
        in_specs=[smem_spec(), smem_spec()] + [vmem_spec()] * (3 + len(pieces)),
        out_specs=(vmem_spec(), vmem_spec()),
        compiler_params=params(16),
        name="push_blocks",
    )(det, pull_index, direction, residual, preconditioner, *pieces)


def update_kernel(
    part_ref, solution_ref, residual_ref, direction_ref, operated_ref, pre_ref, new_solution_ref, new_residual_ref, new_direction_ref
):
    totals = jnp.sum(part_ref[...], axis=0, keepdims=True)
    rz_old, curv_sum, cross, square = (totals[:, place : place + 1] for place in range(4))
    size = rz_old / curv_sum
    ratio = (rz_old - 2.0 * size * cross + size * size * square) / rz_old
    size = jnp.broadcast_to(size, (ROWS, PB))
    ratio = jnp.broadcast_to(ratio, (ROWS, PB))

    def body(index, carry):
        rows = pl.ds(pl.multiple_of(index * ROWS, ROWS), ROWS)
        line = [direction_ref[k, rows, :] for k in range(3)]
        new = [residual_ref[k, rows, :] - size * operated_ref[k, rows, :] for k in range(3)]
        applied = precondition([pre_ref[entry, rows, :] for entry in range(6)], new)
        for k in range(3):
            new_solution_ref[k, rows, :] = solution_ref[k, rows, :] + size * line[k]
            new_residual_ref[k, rows, :] = new[k]
            new_direction_ref[k, rows, :] = applied[k] + ratio * line[k]
        return carry

    lax.fori_loop(0, solution_ref.shape[1] // ROWS, body, 0, unroll=4)


def update_maps(parts, solution, residual, direction, operated, preconditioner, chunk):
    maps = pl.BlockSpec((3, chunk, PB), lambda i: (0, i, 0))
    wide = pl.BlockSpec((6, chunk, PB), lambda i: (0, i, 0))
    return pl.pallas_call(
        update_kernel,
        grid=(solution.shape[1] // chunk,),
        out_shape=(jax.ShapeDtypeStruct(solution.shape, F32),) * 3,
        in_specs=[vmem_spec()] + [maps] * 4 + [wide],
        out_specs=(maps,) * 3,
        compiler_params=params(16),
        name="update_maps",
    )(parts, solution, residual, direction, operated, preconditioner)


def exchanged(value, axis, bit):
    count = lax.axis_size(axis)
    return lax.ppermute(value, axis, [(source, source ^ bit) for source in range(count)])


def delivered(own, other, sign):
    times, dets = lax.axis_size("tm"), lax.axis_size("det")
    got = exchanged(other, "det", 1)
    pieces = []
    for reach in range(own.shape[0]):
        for hop in range(own.shape[1]):
            pair = jnp.stack([own[reach, hop], got[reach, hop]])
            if reach or hop:
                pair = lax.ppermute(
                    pair,
                    ("tm", "det"),
                    [
                        (time * dets + det, (time + sign * reach) % times * dets + (det ^ (2 * hop)))
                        for time in range(times)
                        for det in range(dets)
                    ],
                )
            pieces.append(pair)
    return pieces


def summed_over_det(value):
    count = lax.axis_size("det")
    half = value.shape[1] // 2
    core = lax.axis_index("det") % 2
    own = lax.dynamic_slice_in_dim(value, core * half, half, 1)
    other = lax.dynamic_slice_in_dim(value, (1 - core) * half, half, 1)
    own = own + exchanged(other, "det", 1)
    bit = 2
    while bit < count:
        own = own + exchanged(own, "det", bit)
        bit *= 2
    other = exchanged(own, "det", 1)
    lower = jnp.where(core == 0, own, other)
    upper = jnp.where(core == 0, other, own)
    return jnp.concatenate([lower, upper], axis=1)


def on_device(
    solution,
    residual,
    direction,
    preconditioner,
    pull_index,
    block_slot,
    pixel_offset,
    angle_index,
    det_weight,
    mode_templates,
    mode_precision,
):
    det_dev = pixel_offset.shape[0]
    device_count = lax.axis_size("tm") * lax.axis_size("det")
    det = lax.axis_index("det").astype(jnp.int32)[None]

    own, other = pull_blocks(det, pull_index, direction)
    pieces = delivered(own, other, -1)
    back, weighted, own_weight = mode_matrices(det, det_dev, mode_templates, det_weight, mode_precision)
    timeline, local_proj = make_timeline(
        det, block_slot, weighted, pixel_offset, angle_index, pieces, 2048
    )
    projection = summed_over_det(local_proj)
    own, other = bin_samples(
        det, block_slot, projection, trig_table(), back, own_weight, pixel_offset, angle_index, timeline,
        pull_index.shape[2:], 1024,
    )
    arrived = delivered(own, other, 1)
    operated, parts = push_blocks(
        det, pull_index, direction, residual, preconditioner, arrived, device_count
    )
    parts = lax.all_to_all(parts, ("tm", "det"), split_axis=0, concat_axis=0, tiled=True)
    return update_maps(parts, solution, residual, direction, operated, preconditioner, 96)


def solution(mesh):
    maps = P(None, ("tm", "det"), None)
    samples = P("det", "tm")
    in_specs = (maps,) * 4 + (P("tm", "det", None, None, None),) + (samples,) * 3 + (P(),) * 3
    return jax.shard_map(
        on_device, mesh=mesh, in_specs=in_specs, out_specs=(maps,) * 3, check_vma=False
    )
```

```python
import math

import jax
import jax.numpy as jnp
import numpy as np
from jax import lax
from jax.experimental import pallas as pl
from jax.experimental.pallas import tpu as pltpu
from jax.sharding import PartitionSpec as P

PB = 128
SB = 128
RUN = 4
NANG = 64
GROUP = 8
RUN_LEN = RUN * SB
ROWS = 8
LOW = 32
HIGH = PB // LOW
F32 = jnp.float32
BF16 = jnp.bfloat16
HIGHEST = lax.Precision.HIGHEST
MIB = 1024 * 1024
TERMS = 8


def vmem_spec():
    return pl.BlockSpec(memory_space=pltpu.VMEM)


def smem_spec():
    return pl.BlockSpec(memory_space=pltpu.SMEM)


def in_hbm(*arrays):
    return tuple(pltpu.with_memory_space_constraint(array, pltpu.HBM) for array in arrays)


def params(mib):
    return pltpu.CompilerParams(vmem_limit_bytes=mib * MIB)


def wave_terms():
    turn = (np.arange(NANG) - NANG // 2).astype(np.float64) / NANG
    powers = np.stack([turn ** (2 * term) for term in range(TERMS)], axis=1)
    even = np.linalg.lstsq(powers, -np.cos(2.0 * math.pi * turn), rcond=None)[0]
    odd = np.linalg.lstsq(powers * turn[:, None], -np.sin(2.0 * math.pi * turn), rcond=None)[0]
    return [float(term) for term in even], [float(term) for term in odd]


EVEN_TERMS, ODD_TERMS = wave_terms()


def waves(angle):
    turn = (angle - NANG // 2).astype(F32) * (1.0 / NANG)
    square = turn * turn
    even = jnp.full_like(turn, EVEN_TERMS[-1])
    odd = jnp.full_like(turn, ODD_TERMS[-1])
    for term in range(TERMS - 2, -1, -1):
        even = even * square + EVEN_TERMS[term]
        odd = odd * square + ODD_TERMS[term]
    return even, odd * turn


def trig_table():
    lane = lax.broadcasted_iota(jnp.int32, (GROUP, PB), 1)
    cos_vals, sin_vals = waves(lane & (NANG - 1))
    return jnp.where(lane < NANG, cos_vals, sin_vals)


def halves(value):
    first = value.astype(BF16)
    rest = value - first.astype(F32)
    second = rest.astype(BF16)
    return first, second, (rest - second.astype(F32)).astype(BF16)


def lane_pick(table, index):
    return jnp.take_along_axis(table, index, axis=1, mode="promise_in_bounds")


def wide_pick(table, index):
    parts = [
        lane_pick(table, index[:, PB * part : PB * (part + 1)])
        for part in range(index.shape[1] // PB)
    ]
    return jnp.concatenate(parts, axis=1)


def precondition(pre, field):
    return (
        pre[0] * field[0] + pre[3] * field[1] + pre[4] * field[2],
        pre[3] * field[0] + pre[1] * field[1] + pre[5] * field[2],
        pre[4] * field[0] + pre[5] * field[1] + pre[2] * field[2],
    )


def partner(det, hop, flip):
    return det ^ (2 * hop + flip)


def pull_kernel(det_ref, request_ref, direction_ref, own_ref, other_ref):
    _, _, reach_count, group_count, cap_count = request_ref.shape
    det = det_ref[0]
    for flip, ref in ((1, other_ref), (0, own_ref)):
        for reach in range(reach_count):
            for hop in range(group_count // 2):
                group = partner(det, hop, flip)
                for slot in range(cap_count):
                    block = request_ref[0, 0, reach, group, slot]
                    for k in range(3):
                        ref[reach, hop, pl.ds(k * cap_count + slot, 1), :] = direction_ref[
                            k, pl.ds(block, 1), :
                        ]


def pull_blocks(det, pull_index, direction):
    _, _, reach_count, group_count, cap_count = pull_index.shape
    piece = jax.ShapeDtypeStruct((reach_count, group_count // 2, 3 * cap_count, PB), F32)
    return pl.pallas_call(
        pull_kernel,
        out_shape=(piece, piece),
        in_specs=[smem_spec(), smem_spec(), vmem_spec()],
        out_specs=(vmem_spec(), vmem_spec()),
        compiler_params=params(24),
        name="pull_blocks",
    )(det, *in_hbm(pull_index, direction))


def own_lanes(ref, first, count):
    rows, total = ref.shape
    value = jnp.broadcast_to(ref[...], (max(rows, ROWS), total))
    return pltpu.roll(value, lax.rem(total - first, total), 1)[:, :count]


def mode_kernel(det_ref, template_ref, weight_ref, precision_ref, after_ref, back_ref, own_weight_ref):
    del after_ref
    det_dev = back_ref.shape[0]
    modes = template_ref.shape[0]
    templates = template_ref[...]
    first = det_ref[0] * det_dev
    own_templates = own_lanes(template_ref, first, det_dev)
    own_weight_ref[...] = own_lanes(weight_ref, first, det_dev).T[:, :1]
    row = lax.broadcasted_iota(jnp.int32, (modes, modes), 0)
    column = lax.broadcasted_iota(jnp.int32, (modes, modes), 1)
    unit = (row == column).astype(F32)
    core = unit * precision_ref[...] + lax.dot_general(
        templates * weight_ref[:1, :], templates, (((1,), (1,)), ((), ())), precision=HIGHEST, preferred_element_type=F32
    )
    inverse = unit
    line = lax.broadcasted_iota(jnp.int32, (modes, 1), 0)
    for step in range(modes):
        root = 1.0 / jnp.sqrt(core[step : step + 1, step : step + 1])
        factor = jnp.where(line > step, core[:, step : step + 1] * root, 0.0)
        core_row = core[step : step + 1, :] * root
        inverse_row = inverse[step : step + 1, :] * root
        core = core - factor * core_row
        inverse = jnp.where(line == step, inverse_row, inverse - factor * inverse_row)
    solved = lax.dot_general(
        inverse, inverse, (((0,), (0,)), ((), ())), precision=HIGHEST, preferred_element_type=F32
    )
    back_ref[...] = jnp.dot(solved, own_templates, precision=HIGHEST, preferred_element_type=F32).T


def mode_matrices(det, det_dev, templates, weight, mode_precision, after):
    modes = templates.shape[0]
    return pl.pallas_call(
        mode_kernel,
        out_shape=(
            jax.ShapeDtypeStruct((det_dev, modes), F32),
            jax.ShapeDtypeStruct((det_dev, 1), F32),
        ),
        in_specs=[smem_spec(), vmem_spec(), vmem_spec(), vmem_spec(), pl.BlockSpec(memory_space=pl.ANY)],
        out_specs=(vmem_spec(), vmem_spec()),
        compiler_params=params(8),
        name="mode_matrices",
    )(det, *in_hbm(templates, weight, mode_precision[None, :]), after)


def timeline_kernel(det_ref, slot_ref, template_ref, weight_ref, offset_ref, angle_ref, *refs):
    *piece_refs, time_ref, proj_ref, map_ref, table_ref, weighted_ref = refs
    step = pl.program_id(0)
    cap_count = piece_refs[0].shape[1] // 3
    hop_count = len(piece_refs) // 2
    det_count, chunk = offset_ref.shape
    runs = chunk // RUN_LEN

    @pl.when(step == 0)
    def _():
        det = det_ref[0]
        first = det * det_count
        weighted_ref[...] = own_lanes(template_ref, first, det_count) * own_lanes(weight_ref, first, det_count)[:1, :]
        for place, ref in enumerate(piece_refs):
            reach, hop = place // hop_count, place % hop_count
            for flip in range(2):
                block = (reach * 2 * hop_count + partner(det, hop, flip)) * cap_count
                first = pl.multiple_of(block * ROWS, cap_count * ROWS)
                for k in range(3):
                    map_ref[pl.ds(first + k, cap_count, stride=ROWS), :] = ref[
                        flip, pl.ds(k * cap_count, cap_count), :
                    ]

    def body(group, carry):
        first = pl.multiple_of(group * GROUP, GROUP)
        for run in range(runs):
            for det in range(GROUP):
                slot = slot_ref[first + det, (step * runs + run) * RUN]
                table_ref[run, pl.ds(det * ROWS, ROWS), :] = map_ref[
                    pl.ds(pl.multiple_of(slot * ROWS, ROWS), ROWS), :
                ]
            tables = [table_ref[run, pl.ds(k, GROUP, stride=ROWS), :] for k in range(3)]
            for part in range(RUN):
                lanes = pl.ds(run * RUN_LEN + part * SB, SB)
                offset = offset_ref[pl.ds(first, GROUP), lanes]
                angle = angle_ref[pl.ds(first, GROUP), lanes]
                cos_vals, sin_vals = waves(angle)
                time_ref[pl.ds(first, GROUP), lanes] = (
                    lane_pick(tables[0], offset)
                    + cos_vals * lane_pick(tables[1], offset)
                    + sin_vals * lane_pick(tables[2], offset)
                )
        return carry

    lax.fori_loop(0, det_count // GROUP, body, 0, unroll=4)
    proj_ref[...] = jnp.dot(
        weighted_ref[...], time_ref[...], precision=HIGHEST, preferred_element_type=F32
    )


def make_timeline(det, block_slot, templates, weight, pixel_offset, angle_index, pieces, chunk):
    det_dev, samp_dev = pixel_offset.shape
    modes = templates.shape[0]
    slot_total = len(pieces) * 2 * (pieces[0].shape[1] // 3)
    runs = chunk // RUN_LEN
    wide = pl.BlockSpec((det_dev, chunk), lambda i: (0, i))
    return pl.pallas_call(
        timeline_kernel,
        grid=(samp_dev // chunk,),
        out_shape=(
            pltpu.HBM((det_dev, samp_dev), F32),
            jax.ShapeDtypeStruct((modes, samp_dev), F32),
        ),
        in_specs=[smem_spec(), smem_spec(), vmem_spec(), vmem_spec(), wide, wide] + [vmem_spec()] * len(pieces),
        out_specs=(wide, pl.BlockSpec((modes, chunk), lambda i: (0, i))),
        scratch_shapes=[
            pltpu.VMEM((slot_total * ROWS, PB), F32),
            pltpu.VMEM((runs, GROUP * ROWS, PB), F32),
            pltpu.VMEM((modes, det_dev), F32),
        ],
        compiler_params=params(24),
        name="make_timeline",
    )(det, *in_hbm(block_slot, templates, weight, pixel_offset, angle_index), *pieces)


def bin_kernel(
    det_ref, slot_ref, proj_ref, back_ref, weight_ref, offset_ref, angle_ref, time_ref,
    own_ref, other_ref, map_ref, row_ref, filt_ref,
):
    step = pl.program_id(0)
    reach_count, hop_count, rows, _ = own_ref.shape
    cap_count = rows // 3
    det_count, chunk = offset_ref.shape
    runs = chunk // RUN_LEN

    @pl.when(step == 0)
    def _():
        map_ref[...] = jnp.zeros_like(map_ref)
        row_ref[...] = jnp.zeros_like(row_ref)

    back = halves(back_ref[...])
    proj = halves(proj_ref[...])
    orders = ((0, 0), (0, 1), (1, 0), (0, 2), (1, 1), (2, 0))
    common = jnp.dot(
        jnp.concatenate([back[left] for left, _ in orders], axis=1),
        jnp.concatenate([proj[right] for _, right in orders], axis=0),
        preferred_element_type=F32,
    )
    filt_ref[...] = weight_ref[...] * (time_ref[...] - common)
    trig = trig_table()
    det_iota = lax.broadcasted_iota(jnp.int32, (GROUP, RUN_LEN), 0)
    low_iota = lax.broadcasted_iota(jnp.int32, (LOW, RUN_LEN), 0).astype(F32).astype(BF16)
    row_iota = lax.broadcasted_iota(jnp.int32, (GROUP, PB), 0)
    lane_iota = lax.broadcasted_iota(jnp.int32, (GROUP, PB), 1)
    diagonal = lane_iota // LOW == row_iota % HIGH
    zero = jnp.zeros((), BF16)
    one = jnp.ones((), BF16)

    def body(group, carry):
        first = pl.multiple_of(group * GROUP, GROUP)
        for run in range(runs):
            lanes = pl.ds(run * RUN_LEN, RUN_LEN)
            offset = offset_ref[pl.ds(first, GROUP), lanes]
            angle = angle_ref[pl.ds(first, GROUP), lanes]
            filtered = filt_ref[pl.ds(first, GROUP), lanes]
            cos_vals = wide_pick(trig, angle)
            sin_vals = wide_pick(trig, angle + NANG)
            packed = []
            for value in (filtered, cos_vals * filtered, sin_vals * filtered):
                upper = value.astype(BF16).astype(F32)
                packed.append(jnp.concatenate([upper, value - upper], axis=0).astype(BF16))
            turn = ((offset // LOW) - det_iota) & (HIGH - 1)
            turn = turn.astype(F32)
            turn = jnp.concatenate([turn, turn], axis=0).astype(BF16)
            left = jnp.concatenate(
                [jnp.where(turn == jnp.asarray(j, BF16), value, zero) for j in range(HIGH) for value in packed],
                axis=0,
            )
            low = (offset & (LOW - 1)).astype(F32)
            hots = []
            for det in range(GROUP):
                line = jnp.broadcast_to(low[det : det + 1, :], (LOW, RUN_LEN)).astype(BF16)
                hots.append(jnp.where(line == low_iota, one, zero))
            right = jnp.concatenate(hots, axis=0)
            product = lax.dot_general(
                left, right, (((1,), (1,)), ((), ())), preferred_element_type=F32
            )
            for k in range(3):
                total = None
                for j in range(HIGH):
                    top = (j * 3 + k) * 2 * GROUP
                    pair = product[top : top + GROUP] + product[top + GROUP : top + 2 * GROUP]
                    part = jnp.where(row_iota < HIGH, pair[:, :PB], pair[:, PB:])
                    part = jnp.where(diagonal, part, 0.0)
                    if j:
                        part = pltpu.roll(part, LOW * j, 1)
                    total = part if total is None else total + part
                row_ref[run, pl.ds(k, GROUP, stride=ROWS), :] = total
            for det in range(GROUP):
                slot = slot_ref[first + det, (step * runs + run) * RUN]
                at = pl.ds(pl.multiple_of(slot * ROWS, ROWS), ROWS)
                map_ref[at, :] += row_ref[run, pl.ds(det * ROWS, ROWS), :]
        return carry

    lax.fori_loop(0, det_count // GROUP, body, 0, unroll=8)

    @pl.when(step == pl.num_programs(0) - 1)
    def _():
        det = det_ref[0]
        for flip, ref in ((1, other_ref), (0, own_ref)):
            for reach in range(reach_count):
                for hop in range(hop_count):
                    block = (reach * 2 * hop_count + partner(det, hop, flip)) * cap_count
                    start = pl.multiple_of(block * ROWS, cap_count * ROWS)
                    for k in range(3):
                        ref[reach, hop, pl.ds(k * cap_count, cap_count), :] = map_ref[
                            pl.ds(start + k, cap_count, stride=ROWS), :
                        ]


def bin_samples(
    det, block_slot, projection, back, weight, pixel_offset, angle_index, timeline, shape, chunk
):
    det_dev, samp_dev = pixel_offset.shape
    modes = projection.shape[0]
    reach_count, group_count, cap_count = shape
    slot_total = reach_count * group_count * cap_count
    runs = chunk // RUN_LEN
    wide = pl.BlockSpec((det_dev, chunk), lambda i: (0, i))
    piece = jax.ShapeDtypeStruct((reach_count, group_count // 2, 3 * cap_count, PB), F32)
    return pl.pallas_call(
        bin_kernel,
        grid=(samp_dev // chunk,),
        out_shape=(piece, piece),
        in_specs=[smem_spec(), smem_spec(), pl.BlockSpec((modes, chunk), lambda i: (0, i))]
        + [vmem_spec()] * 2
        + [wide, wide, wide],
        out_specs=(vmem_spec(), vmem_spec()),
        scratch_shapes=[
            pltpu.VMEM((slot_total * ROWS, PB), F32),
            pltpu.VMEM((runs, GROUP * ROWS, PB), F32),
            pltpu.VMEM((det_dev, chunk), F32),
        ],
        compiler_params=params(24),
        name="bin_samples",
    )(
        det, *in_hbm(block_slot), projection, back, weight, *in_hbm(pixel_offset, angle_index, timeline)
    )


def push_kernel(det_ref, request_ref, direction_ref, residual_ref, pre_ref, *refs):
    *piece_refs, operated_ref, part_ref = refs
    cap_count = request_ref.shape[4]
    hop_count = len(piece_refs) // 2
    det = det_ref[0]
    operated_ref[...] = jnp.zeros_like(operated_ref)
    for place, ref in enumerate(piece_refs):
        reach, hop = place // hop_count, place % hop_count
        for flip in range(2):
            group = partner(det, hop, flip)
            sums = []
            for slot in range(cap_count):
                block = request_ref[0, 0, reach, group, slot]
                for k in range(3):
                    line = operated_ref[k, pl.ds(block, 1), :]
                    sums.append((block, k, line + ref[flip, pl.ds(k * cap_count + slot, 1), :]))
            for block, k, line in sums:
                operated_ref[k, pl.ds(block, 1), :] = line

    blocks = operated_ref.shape[1]

    def body(index, totals):
        rows = pl.ds(pl.multiple_of(index * ROWS, ROWS), ROWS)
        pre = [pre_ref[entry, rows, :] for entry in range(6)]
        old = [residual_ref[k, rows, :] for k in range(3)]
        oper = [operated_ref[k, rows, :] for k in range(3)]
        line = [direction_ref[k, rows, :] for k in range(3)]
        old_applied = precondition(pre, old)
        oper_applied = precondition(pre, oper)

        def dot(left, right):
            return left[0] * right[0] + left[1] * right[1] + left[2] * right[2]

        parts = (dot(old, old_applied), dot(line, oper), dot(oper, old_applied), dot(oper, oper_applied))
        return tuple(total + part for total, part in zip(totals, parts))

    nothing = jnp.zeros((ROWS, PB), F32)
    totals = lax.fori_loop(0, blocks // ROWS, body, (nothing,) * 4, unroll=4)
    lane = lax.broadcasted_iota(jnp.int32, part_ref.shape, 1)
    row = jnp.zeros(part_ref.shape, F32)
    for place, total in enumerate(totals):
        value = jnp.sum(jnp.sum(total, axis=0, keepdims=True), axis=1, keepdims=True)
        row = jnp.where(lane == place, value, row)
    part_ref[...] = row


def push_blocks(det, pull_index, direction, residual, preconditioner, pieces, device_count):
    return pl.pallas_call(
        push_kernel,
        out_shape=(
            jax.ShapeDtypeStruct(direction.shape, F32),
            jax.ShapeDtypeStruct((device_count, PB), F32),
        ),
        in_specs=[smem_spec(), smem_spec()] + [vmem_spec()] * (3 + len(pieces)),
        out_specs=(vmem_spec(), vmem_spec()),
        compiler_params=params(16),
        name="push_blocks",
    )(det, pull_index, direction, residual, preconditioner, *pieces)


def update_kernel(
    part_ref, solution_ref, residual_ref, direction_ref, operated_ref, pre_ref, new_solution_ref, new_residual_ref, new_direction_ref
):
    totals = jnp.sum(part_ref[...], axis=0, keepdims=True)
    rz_old, curv_sum, cross, square = (totals[:, place : place + 1] for place in range(4))
    size = rz_old / curv_sum
    ratio = (rz_old - 2.0 * size * cross + size * size * square) / rz_old
    size = jnp.broadcast_to(size, (ROWS, PB))
    ratio = jnp.broadcast_to(ratio, (ROWS, PB))

    chunk = new_solution_ref.shape[1]
    start = pl.program_id(0) * chunk

    def body(index, carry):
        rows = pl.ds(pl.multiple_of(start + index * ROWS, ROWS), ROWS)
        here = pl.ds(pl.multiple_of(index * ROWS, ROWS), ROWS)
        line = [direction_ref[k, rows, :] for k in range(3)]
        new = [residual_ref[k, rows, :] - size * operated_ref[k, rows, :] for k in range(3)]
        applied = precondition([pre_ref[entry, rows, :] for entry in range(6)], new)
        for k in range(3):
            new_solution_ref[k, here, :] = solution_ref[k, rows, :] + size * line[k]
            new_residual_ref[k, here, :] = new[k]
            new_direction_ref[k, here, :] = applied[k] + ratio * line[k]
        return carry

    lax.fori_loop(0, chunk // ROWS, body, 0, unroll=4)


def update_maps(parts, solution, residual, direction, operated, preconditioner, chunk):
    maps = pl.BlockSpec((3, chunk, PB), lambda i: (0, i, 0))
    return pl.pallas_call(
        update_kernel,
        grid=(solution.shape[1] // chunk,),
        out_shape=(jax.ShapeDtypeStruct(solution.shape, F32),) * 3,
        in_specs=[vmem_spec()] * 6,
        out_specs=(maps,) * 3,
        compiler_params=params(16),
        name="update_maps",
    )(parts, solution, residual, direction, operated, preconditioner)


def exchanged(value, axis, bit):
    count = lax.axis_size(axis)
    return lax.ppermute(value, axis, [(source, source ^ bit) for source in range(count)])


def delivered(own, other, sign):
    times, dets = lax.axis_size("tm"), lax.axis_size("det")
    got = exchanged(other, "det", 1)
    pieces = []
    for reach in range(own.shape[0]):
        for hop in range(own.shape[1]):
            pair = jnp.stack([own[reach, hop], got[reach, hop]])
            if reach or hop:
                pair = lax.ppermute(
                    pair,
                    ("tm", "det"),
                    [
                        (time * dets + det, (time + sign * reach) % times * dets + (det ^ (2 * hop)))
                        for time in range(times)
                        for det in range(dets)
                    ],
                )
            pieces.append(pair)
    return pieces


def summed_over_det(value, beside):
    count = lax.axis_size("det")
    half = value.shape[1] // 2
    core = lax.axis_index("det") % 2
    own = lax.dynamic_slice_in_dim(value, core * half, half, 1)
    other = lax.dynamic_slice_in_dim(value, (1 - core) * half, half, 1)
    own = own + exchanged(other, "det", 1)
    bit = 2
    while bit < count:
        own = own + exchanged(own, "det", bit)
        bit *= 2
    own, beside = lax.optimization_barrier((own, beside))
    other = exchanged(own, "det", 1)
    lower = jnp.where(core == 0, own, other)
    upper = jnp.where(core == 0, other, own)
    return jnp.concatenate([lower, upper], axis=1), beside


def on_device(
    solution,
    residual,
    direction,
    preconditioner,
    pull_index,
    block_slot,
    pixel_offset,
    angle_index,
    det_weight,
    mode_templates,
    mode_precision,
):
    det_dev = pixel_offset.shape[0]
    device_count = lax.axis_size("tm") * lax.axis_size("det")
    det = lax.axis_index("det").astype(jnp.int32)[None]
    templates = mode_templates.T
    weight = det_weight[None, :]

    own, other = pull_blocks(det, pull_index, direction)
    pieces = delivered(own, other, -1)
    timeline, local_proj = make_timeline(
        det, block_slot, templates, weight, pixel_offset, angle_index, pieces, 2048
    )
    matrices = mode_matrices(det, det_dev, templates, weight, mode_precision, local_proj)
    projection, (back, own_weight) = summed_over_det(local_proj, matrices)
    own, other = bin_samples(
        det, block_slot, projection, back, own_weight, pixel_offset, angle_index, timeline,
        pull_index.shape[2:], 1024,
    )
    arrived = delivered(own, other, 1)
    operated, parts = push_blocks(
        det, pull_index, direction, residual, preconditioner, arrived, device_count
    )
    parts = lax.all_to_all(parts, ("tm", "det"), split_axis=0, concat_axis=0, tiled=True)
    return update_maps(parts, solution, residual, direction, operated, preconditioner, 96)


def solution(mesh):
    maps = P(None, ("tm", "det"), None)
    samples = P("det", "tm")
    in_specs = (maps,) * 4 + (P("tm", "det", None, None, None),) + (samples,) * 3 + (P(),) * 3
    return jax.shard_map(
        on_device, mesh=mesh, in_specs=in_specs, out_specs=(maps,) * 3, check_vma=False
    )
```

```python
import math

import jax
import jax.numpy as jnp
import numpy as np
from jax import lax
from jax.experimental import pallas as pl
from jax.experimental.pallas import tpu as pltpu
from jax.sharding import PartitionSpec as P

PB = 128
SB = 128
RUN = 4
NANG = 64
GROUP = 8
RUN_LEN = RUN * SB
ROWS = 8
LOW = 32
HIGH = PB // LOW
F32 = jnp.float32
BF16 = jnp.bfloat16
HIGHEST = lax.Precision.HIGHEST
MIB = 1024 * 1024
TERMS = 8


def vmem_spec():
    return pl.BlockSpec(memory_space=pltpu.VMEM)


def smem_spec():
    return pl.BlockSpec(memory_space=pltpu.SMEM)


def in_hbm(*arrays):
    return tuple(pltpu.with_memory_space_constraint(array, pltpu.HBM) for array in arrays)


def params(mib):
    return pltpu.CompilerParams(vmem_limit_bytes=mib * MIB)


def wave_terms():
    turn = (np.arange(NANG) - NANG // 2).astype(np.float64) / NANG
    powers = np.stack([turn ** (2 * term) for term in range(TERMS)], axis=1)
    even = np.linalg.lstsq(powers, -np.cos(2.0 * math.pi * turn), rcond=None)[0]
    odd = np.linalg.lstsq(powers * turn[:, None], -np.sin(2.0 * math.pi * turn), rcond=None)[0]
    return [float(term) for term in even], [float(term) for term in odd]


EVEN_TERMS, ODD_TERMS = wave_terms()


def waves(angle):
    turn = (angle - NANG // 2).astype(F32) * (1.0 / NANG)
    square = turn * turn
    even = jnp.full_like(turn, EVEN_TERMS[-1])
    odd = jnp.full_like(turn, ODD_TERMS[-1])
    for term in range(TERMS - 2, -1, -1):
        even = even * square + EVEN_TERMS[term]
        odd = odd * square + ODD_TERMS[term]
    return even, odd * turn


def trig_table():
    lane = lax.broadcasted_iota(jnp.int32, (GROUP, PB), 1)
    cos_vals, sin_vals = waves(lane & (NANG - 1))
    return jnp.where(lane < NANG, cos_vals, sin_vals)


def halves(value):
    first = value.astype(BF16)
    rest = value - first.astype(F32)
    second = rest.astype(BF16)
    return first, second, (rest - second.astype(F32)).astype(BF16)


def lane_pick(table, index):
    return jnp.take_along_axis(table, index, axis=1, mode="promise_in_bounds")


def wide_pick(table, index):
    parts = [
        lane_pick(table, index[:, PB * part : PB * (part + 1)])
        for part in range(index.shape[1] // PB)
    ]
    return jnp.concatenate(parts, axis=1)


def precondition(pre, field):
    return (
        pre[0] * field[0] + pre[3] * field[1] + pre[4] * field[2],
        pre[3] * field[0] + pre[1] * field[1] + pre[5] * field[2],
        pre[4] * field[0] + pre[5] * field[1] + pre[2] * field[2],
    )


def partner(det, hop, flip):
    return det ^ (2 * hop + flip)


def pull_kernel(det_ref, request_ref, direction_ref, own_ref, other_ref):
    _, _, reach_count, group_count, cap_count = request_ref.shape
    det = det_ref[0]
    for flip, ref in ((1, other_ref), (0, own_ref)):
        for reach in range(reach_count):
            for hop in range(group_count // 2):
                group = partner(det, hop, flip)
                for slot in range(cap_count):
                    block = request_ref[0, 0, reach, group, slot]
                    for k in range(3):
                        ref[reach, hop, pl.ds(k * cap_count + slot, 1), :] = direction_ref[
                            k, pl.ds(block, 1), :
                        ]


def pull_blocks(det, pull_index, direction):
    _, _, reach_count, group_count, cap_count = pull_index.shape
    piece = jax.ShapeDtypeStruct((reach_count, group_count // 2, 3 * cap_count, PB), F32)
    return pl.pallas_call(
        pull_kernel,
        out_shape=(piece, piece),
        in_specs=[smem_spec(), smem_spec(), vmem_spec()],
        out_specs=(vmem_spec(), vmem_spec()),
        compiler_params=params(24),
        name="pull_blocks",
    )(det, *in_hbm(pull_index, direction))


def own_lanes(ref, first, count):
    rows, total = ref.shape
    value = jnp.broadcast_to(ref[...], (max(rows, ROWS), total))
    return pltpu.roll(value, lax.rem(total - first, total), 1)[:, :count]


def mode_kernel(det_ref, template_ref, weight_ref, precision_ref, after_ref, back_ref, own_weight_ref):
    del after_ref
    det_dev = back_ref.shape[0]
    modes = template_ref.shape[0]
    templates = template_ref[...]
    first = det_ref[0] * det_dev
    own_templates = own_lanes(template_ref, first, det_dev)
    own_weight_ref[...] = own_lanes(weight_ref, first, det_dev).T[:, :1]
    row = lax.broadcasted_iota(jnp.int32, (modes, modes), 0)
    column = lax.broadcasted_iota(jnp.int32, (modes, modes), 1)
    unit = (row == column).astype(F32)
    core = unit * precision_ref[...] + lax.dot_general(
        templates * weight_ref[:1, :], templates, (((1,), (1,)), ((), ())), precision=HIGHEST, preferred_element_type=F32
    )
    inverse = unit
    line = lax.broadcasted_iota(jnp.int32, (modes, 1), 0)
    for step in range(modes):
        root = 1.0 / jnp.sqrt(core[step : step + 1, step : step + 1])
        factor = jnp.where(line > step, core[:, step : step + 1] * root, 0.0)
        core_row = core[step : step + 1, :] * root
        inverse_row = inverse[step : step + 1, :] * root
        core = core - factor * core_row
        inverse = jnp.where(line == step, inverse_row, inverse - factor * inverse_row)
    solved = lax.dot_general(
        inverse, inverse, (((0,), (0,)), ((), ())), precision=HIGHEST, preferred_element_type=F32
    )
    back_ref[...] = jnp.dot(solved, own_templates, precision=HIGHEST, preferred_element_type=F32).T


def mode_matrices(det, det_dev, templates, weight, mode_precision, after):
    modes = templates.shape[0]
    return pl.pallas_call(
        mode_kernel,
        out_shape=(
            jax.ShapeDtypeStruct((det_dev, modes), F32),
            jax.ShapeDtypeStruct((det_dev, 1), F32),
        ),
        in_specs=[smem_spec(), vmem_spec(), vmem_spec(), vmem_spec(), pl.BlockSpec(memory_space=pl.ANY)],
        out_specs=(vmem_spec(), vmem_spec()),
        compiler_params=params(8),
        name="mode_matrices",
    )(det, *in_hbm(templates, weight, mode_precision[None, :]), after)


def timeline_kernel(det_ref, slot_ref, template_ref, weight_ref, offset_ref, angle_ref, *refs):
    *piece_refs, time_ref, proj_ref, map_ref, table_ref, weighted_ref = refs
    step = pl.program_id(0)
    cap_count = piece_refs[0].shape[1] // 3
    hop_count = len(piece_refs) // 2
    det_count, chunk = offset_ref.shape
    runs = chunk // RUN_LEN

    @pl.when(step == 0)
    def _():
        det = det_ref[0]
        first = det * det_count
        weighted_ref[...] = own_lanes(template_ref, first, det_count) * own_lanes(weight_ref, first, det_count)[:1, :]
        for place, ref in enumerate(piece_refs):
            reach, hop = place // hop_count, place % hop_count
            for flip in range(2):
                block = (reach * 2 * hop_count + partner(det, hop, flip)) * cap_count
                first = pl.multiple_of(block * ROWS, cap_count * ROWS)
                for k in range(3):
                    map_ref[pl.ds(first + k, cap_count, stride=ROWS), :] = ref[
                        flip, pl.ds(k * cap_count, cap_count), :
                    ]

    def body(group, carry):
        first = pl.multiple_of(group * GROUP, GROUP)
        for run in range(runs):
            for det in range(GROUP):
                slot = slot_ref[first + det, (step * runs + run) * RUN]
                table_ref[run, pl.ds(det * ROWS, ROWS), :] = map_ref[
                    pl.ds(pl.multiple_of(slot * ROWS, ROWS), ROWS), :
                ]
            tables = [table_ref[run, pl.ds(k, GROUP, stride=ROWS), :] for k in range(3)]
            for part in range(RUN):
                lanes = pl.ds(run * RUN_LEN + part * SB, SB)
                offset = offset_ref[pl.ds(first, GROUP), lanes]
                angle = angle_ref[pl.ds(first, GROUP), lanes]
                cos_vals, sin_vals = waves(angle)
                time_ref[pl.ds(first, GROUP), lanes] = (
                    lane_pick(tables[0], offset)
                    + cos_vals * lane_pick(tables[1], offset)
                    + sin_vals * lane_pick(tables[2], offset)
                )
        return carry

    lax.fori_loop(0, det_count // GROUP, body, 0, unroll=8)
    proj_ref[...] = jnp.dot(
        weighted_ref[...], time_ref[...], precision=HIGHEST, preferred_element_type=F32
    )


def make_timeline(det, block_slot, templates, weight, pixel_offset, angle_index, pieces, chunk):
    det_dev, samp_dev = pixel_offset.shape
    modes = templates.shape[0]
    slot_total = len(pieces) * 2 * (pieces[0].shape[1] // 3)
    runs = chunk // RUN_LEN
    wide = pl.BlockSpec((det_dev, chunk), lambda i: (0, i))
    return pl.pallas_call(
        timeline_kernel,
        grid=(samp_dev // chunk,),
        out_shape=(
            pltpu.HBM((det_dev, samp_dev), F32),
            jax.ShapeDtypeStruct((modes, samp_dev), F32),
        ),
        in_specs=[smem_spec(), smem_spec(), vmem_spec(), vmem_spec(), wide, wide] + [vmem_spec()] * len(pieces),
        out_specs=(wide, pl.BlockSpec((modes, chunk), lambda i: (0, i))),
        scratch_shapes=[
            pltpu.VMEM((slot_total * ROWS, PB), F32),
            pltpu.VMEM((runs, GROUP * ROWS, PB), F32),
            pltpu.VMEM((modes, det_dev), F32),
        ],
        compiler_params=params(24),
        name="make_timeline",
    )(det, *in_hbm(block_slot, templates, weight, pixel_offset, angle_index), *pieces)


def bin_kernel(
    det_ref, slot_ref, proj_ref, back_ref, weight_ref, offset_ref, angle_ref, time_ref,
    own_ref, other_ref, map_ref, row_ref, filt_ref,
):
    step = pl.program_id(0)
    reach_count, hop_count, rows, _ = own_ref.shape
    cap_count = rows // 3
    det_count, chunk = offset_ref.shape
    runs = chunk // RUN_LEN

    @pl.when(step == 0)
    def _():
        map_ref[...] = jnp.zeros_like(map_ref)
        row_ref[...] = jnp.zeros_like(row_ref)

    back = halves(back_ref[...])
    proj = halves(proj_ref[...])
    orders = ((0, 0), (0, 1), (1, 0), (0, 2), (1, 1), (2, 0))
    common = jnp.dot(
        jnp.concatenate([back[left] for left, _ in orders], axis=1),
        jnp.concatenate([proj[right] for _, right in orders], axis=0),
        preferred_element_type=F32,
    )
    filt_ref[...] = weight_ref[...] * (time_ref[...] - common)
    trig = trig_table()
    det_iota = lax.broadcasted_iota(jnp.int32, (GROUP, RUN_LEN), 0)
    low_iota = lax.broadcasted_iota(jnp.int32, (LOW, RUN_LEN), 0).astype(F32).astype(BF16)
    row_iota = lax.broadcasted_iota(jnp.int32, (GROUP, PB), 0)
    lane_iota = lax.broadcasted_iota(jnp.int32, (GROUP, PB), 1)
    places = [((lane_iota // LOW) - row_iota - j) % HIGH == 0 for j in range(HIGH)]
    zero = jnp.zeros((), BF16)
    one = jnp.ones((), BF16)

    def body(group, carry):
        first = pl.multiple_of(group * GROUP, GROUP)
        for run in range(runs):
            lanes = pl.ds(run * RUN_LEN, RUN_LEN)
            offset = offset_ref[pl.ds(first, GROUP), lanes]
            angle = angle_ref[pl.ds(first, GROUP), lanes]
            filtered = filt_ref[pl.ds(first, GROUP), lanes]
            cos_vals = wide_pick(trig, angle)
            sin_vals = wide_pick(trig, angle + NANG)
            packed = []
            for value in (filtered, cos_vals * filtered, sin_vals * filtered):
                upper = value.astype(BF16).astype(F32)
                packed.append(jnp.concatenate([upper, value - upper], axis=0).astype(BF16))
            turn = ((offset // LOW) - det_iota) & (HIGH - 1)
            turn = turn.astype(F32)
            turn = jnp.concatenate([turn, turn], axis=0).astype(BF16)
            left = jnp.concatenate(
                [jnp.where(turn == jnp.asarray(j, BF16), value, zero) for j in range(HIGH) for value in packed],
                axis=0,
            )
            low = (offset & (LOW - 1)).astype(F32)
            hots = []
            for det in range(GROUP):
                line = jnp.broadcast_to(low[det : det + 1, :], (LOW, RUN_LEN)).astype(BF16)
                hots.append(jnp.where(line == low_iota, one, zero))
            right = jnp.concatenate(hots, axis=0)
            product = lax.dot_general(
                left, right, (((1,), (1,)), ((), ())), preferred_element_type=F32
            )
            for k in range(3):
                total = None
                for j in range(HIGH):
                    top = (j * 3 + k) * 2 * GROUP
                    pair = product[top : top + GROUP] + product[top + GROUP : top + 2 * GROUP]
                    part = jnp.where(row_iota < HIGH, pair[:, :PB], pair[:, PB:])
                    if j:
                        part = pltpu.roll(part, LOW * j, 1)
                    total = part if total is None else jnp.where(places[j], part, total)
                row_ref[run, pl.ds(k, GROUP, stride=ROWS), :] = total
            for det in range(GROUP):
                slot = slot_ref[first + det, (step * runs + run) * RUN]
                at = pl.ds(pl.multiple_of(slot * ROWS, ROWS), ROWS)
                map_ref[at, :] += row_ref[run, pl.ds(det * ROWS, ROWS), :]
        return carry

    lax.fori_loop(0, det_count // GROUP, body, 0, unroll=8)

    @pl.when(step == pl.num_programs(0) - 1)
    def _():
        det = det_ref[0]
        for flip, ref in ((1, other_ref), (0, own_ref)):
            for reach in range(reach_count):
                for hop in range(hop_count):
                    block = (reach * 2 * hop_count + partner(det, hop, flip)) * cap_count
                    start = pl.multiple_of(block * ROWS, cap_count * ROWS)
                    for k in range(3):
                        ref[reach, hop, pl.ds(k * cap_count, cap_count), :] = map_ref[
                            pl.ds(start + k, cap_count, stride=ROWS), :
                        ]


def bin_samples(
    det, block_slot, projection, back, weight, pixel_offset, angle_index, timeline, shape, chunk
):
    det_dev, samp_dev = pixel_offset.shape
    modes = projection.shape[0]
    reach_count, group_count, cap_count = shape
    slot_total = reach_count * group_count * cap_count
    runs = chunk // RUN_LEN
    wide = pl.BlockSpec((det_dev, chunk), lambda i: (0, i))
    piece = jax.ShapeDtypeStruct((reach_count, group_count // 2, 3 * cap_count, PB), F32)
    return pl.pallas_call(
        bin_kernel,
        grid=(samp_dev // chunk,),
        out_shape=(piece, piece),
        in_specs=[smem_spec(), smem_spec(), pl.BlockSpec((modes, chunk), lambda i: (0, i))]
        + [vmem_spec()] * 2
        + [wide, wide, wide],
        out_specs=(vmem_spec(), vmem_spec()),
        scratch_shapes=[
            pltpu.VMEM((slot_total * ROWS, PB), F32),
            pltpu.VMEM((runs, GROUP * ROWS, PB), F32),
            pltpu.VMEM((det_dev, chunk), F32),
        ],
        compiler_params=params(24),
        name="bin_samples",
    )(
        det, *in_hbm(block_slot), projection, back, weight, *in_hbm(pixel_offset, angle_index, timeline)
    )


def push_kernel(det_ref, request_ref, direction_ref, residual_ref, pre_ref, *refs):
    *piece_refs, operated_ref, part_ref = refs
    cap_count = request_ref.shape[4]
    hop_count = len(piece_refs) // 2
    det = det_ref[0]
    operated_ref[...] = jnp.zeros_like(operated_ref)
    for place, ref in enumerate(piece_refs):
        reach, hop = place // hop_count, place % hop_count
        for flip in range(2):
            group = partner(det, hop, flip)
            sums = []
            for slot in range(cap_count):
                block = request_ref[0, 0, reach, group, slot]
                for k in range(3):
                    line = operated_ref[k, pl.ds(block, 1), :]
                    sums.append((block, k, line + ref[flip, pl.ds(k * cap_count + slot, 1), :]))
            for block, k, line in sums:
                operated_ref[k, pl.ds(block, 1), :] = line

    blocks = operated_ref.shape[1]

    def body(index, totals):
        rows = pl.ds(pl.multiple_of(index * ROWS, ROWS), ROWS)
        pre = [pre_ref[entry, rows, :] for entry in range(6)]
        old = [residual_ref[k, rows, :] for k in range(3)]
        oper = [operated_ref[k, rows, :] for k in range(3)]
        line = [direction_ref[k, rows, :] for k in range(3)]
        old_applied = precondition(pre, old)
        oper_applied = precondition(pre, oper)

        def dot(left, right):
            return left[0] * right[0] + left[1] * right[1] + left[2] * right[2]

        parts = (dot(old, old_applied), dot(line, oper), dot(oper, old_applied), dot(oper, oper_applied))
        return tuple(total + part for total, part in zip(totals, parts))

    nothing = jnp.zeros((ROWS, PB), F32)
    totals = lax.fori_loop(0, blocks // ROWS, body, (nothing,) * 4, unroll=4)
    lane = lax.broadcasted_iota(jnp.int32, part_ref.shape, 1)
    row = jnp.zeros(part_ref.shape, F32)
    for place, total in enumerate(totals):
        value = jnp.sum(jnp.sum(total, axis=0, keepdims=True), axis=1, keepdims=True)
        row = jnp.where(lane == place, value, row)
    part_ref[...] = row


def push_blocks(det, pull_index, direction, residual, preconditioner, pieces, device_count):
    return pl.pallas_call(
        push_kernel,
        out_shape=(
            jax.ShapeDtypeStruct(direction.shape, F32),
            jax.ShapeDtypeStruct((device_count, PB), F32),
        ),
        in_specs=[smem_spec(), smem_spec()] + [vmem_spec()] * (3 + len(pieces)),
        out_specs=(vmem_spec(), vmem_spec()),
        compiler_params=params(16),
        name="push_blocks",
    )(det, pull_index, direction, residual, preconditioner, *pieces)


def update_kernel(
    part_ref, solution_ref, residual_ref, direction_ref, operated_ref, pre_ref, new_solution_ref, new_residual_ref, new_direction_ref
):
    totals = jnp.sum(part_ref[...], axis=0, keepdims=True)
    rz_old, curv_sum, cross, square = (totals[:, place : place + 1] for place in range(4))
    size = rz_old / curv_sum
    ratio = (rz_old - 2.0 * size * cross + size * size * square) / rz_old
    size = jnp.broadcast_to(size, (ROWS, PB))
    ratio = jnp.broadcast_to(ratio, (ROWS, PB))

    chunk = new_solution_ref.shape[1]
    start = pl.program_id(0) * chunk

    def body(index, carry):
        rows = pl.ds(pl.multiple_of(start + index * ROWS, ROWS), ROWS)
        here = pl.ds(pl.multiple_of(index * ROWS, ROWS), ROWS)
        line = [direction_ref[k, rows, :] for k in range(3)]
        new = [residual_ref[k, rows, :] - size * operated_ref[k, rows, :] for k in range(3)]
        applied = precondition([pre_ref[entry, rows, :] for entry in range(6)], new)
        for k in range(3):
            new_solution_ref[k, here, :] = solution_ref[k, rows, :] + size * line[k]
            new_residual_ref[k, here, :] = new[k]
            new_direction_ref[k, here, :] = applied[k] + ratio * line[k]
        return carry

    lax.fori_loop(0, chunk // ROWS, body, 0, unroll=4)


def update_maps(parts, solution, residual, direction, operated, preconditioner, chunk):
    maps = pl.BlockSpec((3, chunk, PB), lambda i: (0, i, 0))
    return pl.pallas_call(
        update_kernel,
        grid=(solution.shape[1] // chunk,),
        out_shape=(jax.ShapeDtypeStruct(solution.shape, F32),) * 3,
        in_specs=[vmem_spec()] * 6,
        out_specs=(maps,) * 3,
        compiler_params=params(16),
        name="update_maps",
    )(parts, solution, residual, direction, operated, preconditioner)


def exchanged(value, axis, bit):
    count = lax.axis_size(axis)
    return lax.ppermute(value, axis, [(source, source ^ bit) for source in range(count)])


def delivered(own, other, sign):
    times, dets = lax.axis_size("tm"), lax.axis_size("det")
    got = exchanged(other, "det", 1)
    pieces = []
    for reach in range(own.shape[0]):
        for hop in range(own.shape[1]):
            pair = jnp.stack([own[reach, hop], got[reach, hop]])
            if reach or hop:
                pair = lax.ppermute(
                    pair,
                    ("tm", "det"),
                    [
                        (time * dets + det, (time + sign * reach) % times * dets + (det ^ (2 * hop)))
                        for time in range(times)
                        for det in range(dets)
                    ],
                )
            pieces.append(pair)
    return pieces


def summed_over_det(value, beside):
    count = lax.axis_size("det")
    half = value.shape[1] // 2
    core = lax.axis_index("det") % 2
    own = lax.dynamic_slice_in_dim(value, core * half, half, 1)
    other = lax.dynamic_slice_in_dim(value, (1 - core) * half, half, 1)
    own = own + exchanged(other, "det", 1)
    bit = 2
    while bit < count:
        own = own + exchanged(own, "det", bit)
        bit *= 2
    own, beside = lax.optimization_barrier((own, beside))
    other = exchanged(own, "det", 1)
    lower = jnp.where(core == 0, own, other)
    upper = jnp.where(core == 0, other, own)
    return jnp.concatenate([lower, upper], axis=1), beside


def on_device(
    solution,
    residual,
    direction,
    preconditioner,
    pull_index,
    block_slot,
    pixel_offset,
    angle_index,
    det_weight,
    mode_templates,
    mode_precision,
):
    det_dev = pixel_offset.shape[0]
    device_count = lax.axis_size("tm") * lax.axis_size("det")
    det = lax.axis_index("det").astype(jnp.int32)[None]
    templates = mode_templates.T
    weight = det_weight[None, :]

    own, other = pull_blocks(det, pull_index, direction)
    pieces = delivered(own, other, -1)
    timeline, local_proj = make_timeline(
        det, block_slot, templates, weight, pixel_offset, angle_index, pieces, 2048
    )
    matrices = mode_matrices(det, det_dev, templates, weight, mode_precision, local_proj)
    projection, (back, own_weight) = summed_over_det(local_proj, matrices)
    own, other = bin_samples(
        det, block_slot, projection, back, own_weight, pixel_offset, angle_index, timeline,
        pull_index.shape[2:], 2048,
    )
    arrived = delivered(own, other, 1)
    operated, parts = push_blocks(
        det, pull_index, direction, residual, preconditioner, arrived, device_count
    )
    parts = lax.all_to_all(parts, ("tm", "det"), split_axis=0, concat_axis=0, tiled=True)
    return update_maps(parts, solution, residual, direction, operated, preconditioner, 96)


def solution(mesh):
    maps = P(None, ("tm", "det"), None)
    samples = P("det", "tm")
    in_specs = (maps,) * 4 + (P("tm", "det", None, None, None),) + (samples,) * 3 + (P(),) * 3
    return jax.shard_map(
        on_device, mesh=mesh, in_specs=in_specs, out_specs=(maps,) * 3, check_vma=False
    )
```

```python
import math

import jax
import jax.numpy as jnp
import numpy as np
from jax import lax
from jax.experimental import pallas as pl
from jax.experimental.pallas import tpu as pltpu
from jax.sharding import PartitionSpec as P

PB = 128
SB = 128
RUN = 4
NANG = 64
GROUP = 8
RUN_LEN = RUN * SB
ROWS = 8
LOW = 32
HIGH = PB // LOW
F32 = jnp.float32
BF16 = jnp.bfloat16
HIGHEST = lax.Precision.HIGHEST
MIB = 1024 * 1024
TERMS = 8


def vmem_spec():
    return pl.BlockSpec(memory_space=pltpu.VMEM)


def smem_spec():
    return pl.BlockSpec(memory_space=pltpu.SMEM)


def in_hbm(*arrays):
    return tuple(pltpu.with_memory_space_constraint(array, pltpu.HBM) for array in arrays)


def params(mib):
    return pltpu.CompilerParams(vmem_limit_bytes=mib * MIB)


def wave_terms():
    turn = (np.arange(NANG) - NANG // 2).astype(np.float64) / NANG
    powers = np.stack([turn ** (2 * term) for term in range(TERMS)], axis=1)
    even = np.linalg.lstsq(powers, -np.cos(2.0 * math.pi * turn), rcond=None)[0]
    odd = np.linalg.lstsq(powers * turn[:, None], -np.sin(2.0 * math.pi * turn), rcond=None)[0]
    return [float(term) for term in even], [float(term) for term in odd]


EVEN_TERMS, ODD_TERMS = wave_terms()


def waves(angle):
    turn = (angle - NANG // 2).astype(F32) * (1.0 / NANG)
    square = turn * turn
    even = jnp.full_like(turn, EVEN_TERMS[-1])
    odd = jnp.full_like(turn, ODD_TERMS[-1])
    for term in range(TERMS - 2, -1, -1):
        even = even * square + EVEN_TERMS[term]
        odd = odd * square + ODD_TERMS[term]
    return even, odd * turn


def trig_table():
    lane = lax.broadcasted_iota(jnp.int32, (GROUP, PB), 1)
    cos_vals, sin_vals = waves(lane & (NANG - 1))
    return jnp.where(lane < NANG, cos_vals, sin_vals)


def halves(value):
    first = value.astype(BF16)
    rest = value - first.astype(F32)
    second = rest.astype(BF16)
    return first, second, (rest - second.astype(F32)).astype(BF16)


def lane_pick(table, index):
    return jnp.take_along_axis(table, index, axis=1, mode="promise_in_bounds")


def wide_pick(table, index):
    parts = [
        lane_pick(table, index[:, PB * part : PB * (part + 1)])
        for part in range(index.shape[1] // PB)
    ]
    return jnp.concatenate(parts, axis=1)


def precondition(pre, field):
    return (
        pre[0] * field[0] + pre[3] * field[1] + pre[4] * field[2],
        pre[3] * field[0] + pre[1] * field[1] + pre[5] * field[2],
        pre[4] * field[0] + pre[5] * field[1] + pre[2] * field[2],
    )


def partner(det, hop, flip):
    return det ^ (2 * hop + flip)


def pull_kernel(det_ref, request_ref, direction_ref, own_ref, other_ref):
    _, _, reach_count, group_count, cap_count = request_ref.shape
    det = det_ref[0]
    for flip, ref in ((1, other_ref), (0, own_ref)):
        for reach in range(reach_count):
            for hop in range(group_count // 2):
                group = partner(det, hop, flip)
                for slot in range(cap_count):
                    block = request_ref[0, 0, reach, group, slot]
                    for k in range(3):
                        ref[reach, hop, pl.ds(k * cap_count + slot, 1), :] = direction_ref[
                            k, pl.ds(block, 1), :
                        ]


def pull_blocks(det, pull_index, direction):
    _, _, reach_count, group_count, cap_count = pull_index.shape
    piece = jax.ShapeDtypeStruct((reach_count, group_count // 2, 3 * cap_count, PB), F32)
    return pl.pallas_call(
        pull_kernel,
        out_shape=(piece, piece),
        in_specs=[smem_spec(), smem_spec(), vmem_spec()],
        out_specs=(vmem_spec(), vmem_spec()),
        compiler_params=params(24),
        name="pull_blocks",
    )(det, *in_hbm(pull_index, direction))


def own_lanes(ref, first, count):
    rows, total = ref.shape
    value = jnp.broadcast_to(ref[...], (max(rows, ROWS), total))
    return pltpu.roll(value, lax.rem(total - first, total), 1)[:, :count]


def mode_kernel(det_ref, template_ref, weight_ref, precision_ref, after_ref, back_ref, own_weight_ref):
    del after_ref
    det_dev = back_ref.shape[0]
    modes = template_ref.shape[0]
    templates = template_ref[...]
    first = det_ref[0] * det_dev
    own_templates = own_lanes(template_ref, first, det_dev)
    own_weight_ref[...] = own_lanes(weight_ref, first, det_dev).T[:, :1]
    row = lax.broadcasted_iota(jnp.int32, (modes, modes), 0)
    column = lax.broadcasted_iota(jnp.int32, (modes, modes), 1)
    unit = (row == column).astype(F32)
    core = unit * precision_ref[...] + lax.dot_general(
        templates * weight_ref[:1, :], templates, (((1,), (1,)), ((), ())), precision=HIGHEST, preferred_element_type=F32
    )
    inverse = unit
    line = lax.broadcasted_iota(jnp.int32, (modes, 1), 0)
    for step in range(modes):
        root = 1.0 / jnp.sqrt(core[step : step + 1, step : step + 1])
        factor = jnp.where(line > step, core[:, step : step + 1] * root, 0.0)
        core_row = core[step : step + 1, :] * root
        inverse_row = inverse[step : step + 1, :] * root
        core = core - factor * core_row
        inverse = jnp.where(line == step, inverse_row, inverse - factor * inverse_row)
    solved = lax.dot_general(
        inverse, inverse, (((0,), (0,)), ((), ())), precision=HIGHEST, preferred_element_type=F32
    )
    back_ref[...] = jnp.dot(solved, own_templates, precision=HIGHEST, preferred_element_type=F32).T


def mode_matrices(det, det_dev, templates, weight, mode_precision, after):
    modes = templates.shape[0]
    return pl.pallas_call(
        mode_kernel,
        out_shape=(
            jax.ShapeDtypeStruct((det_dev, modes), F32),
            jax.ShapeDtypeStruct((det_dev, 1), F32),
        ),
        in_specs=[smem_spec(), vmem_spec(), vmem_spec(), vmem_spec(), pl.BlockSpec(memory_space=pl.ANY)],
        out_specs=(vmem_spec(), vmem_spec()),
        compiler_params=params(8),
        name="mode_matrices",
    )(det, *in_hbm(templates, weight, mode_precision[None, :]), after)


def timeline_kernel(det_ref, slot_ref, template_ref, weight_ref, offset_ref, angle_ref, *refs):
    *piece_refs, time_ref, proj_ref, map_ref, table_ref, weighted_ref = refs
    step = pl.program_id(0)
    cap_count = piece_refs[0].shape[1] // 3
    hop_count = len(piece_refs) // 2
    det_count, chunk = offset_ref.shape
    runs = chunk // RUN_LEN

    @pl.when(step == 0)
    def _():
        det = det_ref[0]
        first = det * det_count
        weighted_ref[...] = own_lanes(template_ref, first, det_count) * own_lanes(weight_ref, first, det_count)[:1, :]
        for place, ref in enumerate(piece_refs):
            reach, hop = place // hop_count, place % hop_count
            for flip in range(2):
                block = (reach * 2 * hop_count + partner(det, hop, flip)) * cap_count
                first = pl.multiple_of(block * ROWS, cap_count * ROWS)
                for k in range(3):
                    map_ref[pl.ds(first + k, cap_count, stride=ROWS), :] = ref[
                        flip, pl.ds(k * cap_count, cap_count), :
                    ]

    def body(group, carry):
        first = pl.multiple_of(group * GROUP, GROUP)
        for run in range(runs):
            for det in range(GROUP):
                slot = slot_ref[first + det, (step * runs + run) * RUN]
                table_ref[run, pl.ds(det * ROWS, ROWS), :] = map_ref[
                    pl.ds(pl.multiple_of(slot * ROWS, ROWS), ROWS), :
                ]
            tables = [table_ref[run, pl.ds(k, GROUP, stride=ROWS), :] for k in range(3)]
            for part in range(RUN):
                lanes = pl.ds(run * RUN_LEN + part * SB, SB)
                offset = offset_ref[pl.ds(first, GROUP), lanes]
                angle = angle_ref[pl.ds(first, GROUP), lanes]
                cos_vals, sin_vals = waves(angle)
                time_ref[pl.ds(first, GROUP), lanes] = (
                    lane_pick(tables[0], offset)
                    + cos_vals * lane_pick(tables[1], offset)
                    + sin_vals * lane_pick(tables[2], offset)
                )
        return carry

    lax.fori_loop(0, det_count // GROUP, body, 0, unroll=8)
    proj_ref[...] = jnp.dot(
        weighted_ref[...], time_ref[...], precision=HIGHEST, preferred_element_type=F32
    )


def make_timeline(det, block_slot, templates, weight, pixel_offset, angle_index, pieces, chunk):
    det_dev, samp_dev = pixel_offset.shape
    modes = templates.shape[0]
    slot_total = len(pieces) * 2 * (pieces[0].shape[1] // 3)
    runs = chunk // RUN_LEN
    wide = pl.BlockSpec((det_dev, chunk), lambda i: (0, i))
    return pl.pallas_call(
        timeline_kernel,
        grid=(samp_dev // chunk,),
        out_shape=(
            pltpu.HBM((det_dev, samp_dev), F32),
            jax.ShapeDtypeStruct((modes, samp_dev), F32),
        ),
        in_specs=[smem_spec(), smem_spec(), vmem_spec(), vmem_spec(), wide, wide] + [vmem_spec()] * len(pieces),
        out_specs=(wide, pl.BlockSpec((modes, chunk), lambda i: (0, i))),
        scratch_shapes=[
            pltpu.VMEM((slot_total * ROWS, PB), F32),
            pltpu.VMEM((runs, GROUP * ROWS, PB), F32),
            pltpu.VMEM((modes, det_dev), F32),
        ],
        compiler_params=params(24),
        name="make_timeline",
    )(det, *in_hbm(block_slot, templates, weight, pixel_offset, angle_index), *pieces)


def bin_kernel(
    det_ref, slot_ref, proj_ref, back_ref, weight_ref, offset_ref, angle_ref, time_ref,
    own_ref, other_ref, map_ref, row_ref, filt_ref,
):
    step = pl.program_id(0)
    reach_count, hop_count, rows, _ = own_ref.shape
    cap_count = rows // 3
    det_count, chunk = offset_ref.shape
    runs = chunk // RUN_LEN

    @pl.when(step == 0)
    def _():
        map_ref[...] = jnp.zeros_like(map_ref)
        row_ref[...] = jnp.zeros_like(row_ref)

    back = halves(back_ref[...])
    proj = halves(proj_ref[...])
    orders = ((0, 0), (0, 1), (1, 0), (0, 2), (1, 1), (2, 0))
    common = jnp.dot(
        jnp.concatenate([back[left] for left, _ in orders], axis=1),
        jnp.concatenate([proj[right] for _, right in orders], axis=0),
        preferred_element_type=F32,
    )
    filt_ref[...] = weight_ref[...] * (time_ref[...] - common)
    trig = trig_table()
    det_iota = lax.broadcasted_iota(jnp.int32, (GROUP, RUN_LEN), 0)
    low_iota = lax.broadcasted_iota(jnp.int32, (LOW, RUN_LEN), 0).astype(F32).astype(BF16)
    row_iota = lax.broadcasted_iota(jnp.int32, (GROUP, PB), 0)
    lane_iota = lax.broadcasted_iota(jnp.int32, (GROUP, PB), 1)
    places = [((lane_iota // LOW) - row_iota - j) % HIGH == 0 for j in range(HIGH)]
    zero = jnp.zeros((), BF16)
    one = jnp.ones((), BF16)

    def body(group, carry):
        first = pl.multiple_of(group * GROUP, GROUP)
        for run in range(runs):
            lanes = pl.ds(run * RUN_LEN, RUN_LEN)
            offset = offset_ref[pl.ds(first, GROUP), lanes]
            angle = angle_ref[pl.ds(first, GROUP), lanes]
            filtered = filt_ref[pl.ds(first, GROUP), lanes]
            cos_vals = wide_pick(trig, angle)
            sin_vals = wide_pick(trig, angle + NANG)
            packed = []
            for value in (filtered, cos_vals * filtered, sin_vals * filtered):
                upper = value.astype(BF16).astype(F32)
                packed.append(jnp.concatenate([upper, value - upper], axis=0).astype(BF16))
            turn = ((offset // LOW) - det_iota) & (HIGH - 1)
            turn = turn.astype(F32)
            turn = jnp.concatenate([turn, turn], axis=0).astype(BF16)
            left = jnp.concatenate(
                [jnp.where(turn == jnp.asarray(j, BF16), value, zero) for j in range(HIGH) for value in packed],
                axis=0,
            )
            low = (offset & (LOW - 1)).astype(F32)
            hots = []
            for det in range(GROUP):
                line = jnp.broadcast_to(low[det : det + 1, :], (LOW, RUN_LEN)).astype(BF16)
                hots.append(jnp.where(line == low_iota, one, zero))
            right = jnp.concatenate(hots, axis=0)
            product = lax.dot_general(
                left, right, (((1,), (1,)), ((), ())), preferred_element_type=F32
            )
            for k in range(3):
                total = None
                for j in range(HIGH):
                    top = (j * 3 + k) * 2 * GROUP
                    pair = product[top : top + GROUP] + product[top + GROUP : top + 2 * GROUP]
                    part = jnp.where(row_iota < HIGH, pair[:, :PB], pair[:, PB:])
                    if j:
                        part = pltpu.roll(part, LOW * j, 1)
                    total = part if total is None else jnp.where(places[j], part, total)
                row_ref[run, pl.ds(k, GROUP, stride=ROWS), :] = total
            for det in range(GROUP):
                slot = slot_ref[first + det, (step * runs + run) * RUN]
                at = pl.ds(pl.multiple_of(slot * ROWS, ROWS), ROWS)
                map_ref[at, :] += row_ref[run, pl.ds(det * ROWS, ROWS), :]
        return carry

    lax.fori_loop(0, det_count // GROUP, body, 0, unroll=8)

    @pl.when(step == pl.num_programs(0) - 1)
    def _():
        det = det_ref[0]
        for flip, ref in ((1, other_ref), (0, own_ref)):
            for reach in range(reach_count):
                for hop in range(hop_count):
                    block = (reach * 2 * hop_count + partner(det, hop, flip)) * cap_count
                    start = pl.multiple_of(block * ROWS, cap_count * ROWS)
                    for k in range(3):
                        ref[reach, hop, pl.ds(k * cap_count, cap_count), :] = map_ref[
                            pl.ds(start + k, cap_count, stride=ROWS), :
                        ]


def bin_samples(
    det, block_slot, projection, back, weight, pixel_offset, angle_index, timeline, shape, chunk
):
    det_dev, samp_dev = pixel_offset.shape
    modes = projection.shape[0]
    reach_count, group_count, cap_count = shape
    slot_total = reach_count * group_count * cap_count
    runs = chunk // RUN_LEN
    wide = pl.BlockSpec((det_dev, chunk), lambda i: (0, i))
    piece = jax.ShapeDtypeStruct((reach_count, group_count // 2, 3 * cap_count, PB), F32)
    return pl.pallas_call(
        bin_kernel,
        grid=(samp_dev // chunk,),
        out_shape=(piece, piece),
        in_specs=[smem_spec(), smem_spec(), pl.BlockSpec((modes, chunk), lambda i: (0, i))]
        + [vmem_spec()] * 2
        + [wide, wide, wide],
        out_specs=(vmem_spec(), vmem_spec()),
        scratch_shapes=[
            pltpu.VMEM((slot_total * ROWS, PB), F32),
            pltpu.VMEM((runs, GROUP * ROWS, PB), F32),
            pltpu.VMEM((det_dev, chunk), F32),
        ],
        compiler_params=params(24),
        name="bin_samples",
    )(
        det, *in_hbm(block_slot), projection, back, weight, *in_hbm(pixel_offset, angle_index, timeline)
    )


def push_kernel(det_ref, request_ref, direction_ref, residual_ref, pre_ref, *refs):
    *piece_refs, operated_ref, part_ref = refs
    cap_count = request_ref.shape[4]
    hop_count = len(piece_refs) // 2
    det = det_ref[0]
    operated_ref[...] = jnp.zeros_like(operated_ref)
    for place, ref in enumerate(piece_refs):
        reach, hop = place // hop_count, place % hop_count
        for flip in range(2):
            group = partner(det, hop, flip)
            sums = []
            for slot in range(cap_count):
                block = request_ref[0, 0, reach, group, slot]
                for k in range(3):
                    line = operated_ref[k, pl.ds(block, 1), :]
                    sums.append((block, k, line + ref[flip, pl.ds(k * cap_count + slot, 1), :]))
            for block, k, line in sums:
                operated_ref[k, pl.ds(block, 1), :] = line

    blocks = operated_ref.shape[1]

    def body(index, totals):
        rows = pl.ds(pl.multiple_of(index * ROWS, ROWS), ROWS)
        pre = [pre_ref[entry, rows, :] for entry in range(6)]
        old = [residual_ref[k, rows, :] for k in range(3)]
        oper = [operated_ref[k, rows, :] for k in range(3)]
        line = [direction_ref[k, rows, :] for k in range(3)]
        old_applied = precondition(pre, old)
        oper_applied = precondition(pre, oper)

        def dot(left, right):
            return left[0] * right[0] + left[1] * right[1] + left[2] * right[2]

        parts = (dot(old, old_applied), dot(line, oper), dot(oper, old_applied), dot(oper, oper_applied))
        return tuple(total + part for total, part in zip(totals, parts))

    nothing = jnp.zeros((ROWS, PB), F32)
    totals = lax.fori_loop(0, blocks // ROWS, body, (nothing,) * 4, unroll=8)
    lane = lax.broadcasted_iota(jnp.int32, part_ref.shape, 1)
    row = jnp.zeros(part_ref.shape, F32)
    for place, total in enumerate(totals):
        value = jnp.sum(jnp.sum(total, axis=0, keepdims=True), axis=1, keepdims=True)
        row = jnp.where(lane == place, value, row)
    part_ref[...] = row


def push_blocks(det, pull_index, direction, residual, preconditioner, pieces, device_count):
    return pl.pallas_call(
        push_kernel,
        out_shape=(
            jax.ShapeDtypeStruct(direction.shape, F32),
            jax.ShapeDtypeStruct((device_count, PB), F32),
        ),
        in_specs=[smem_spec(), smem_spec()] + [vmem_spec()] * (3 + len(pieces)),
        out_specs=(vmem_spec(), vmem_spec()),
        compiler_params=params(16),
        name="push_blocks",
    )(det, pull_index, direction, residual, preconditioner, *pieces)


def update_kernel(
    part_ref, solution_ref, residual_ref, direction_ref, operated_ref, pre_ref, new_solution_ref, new_residual_ref, new_direction_ref
):
    totals = jnp.sum(part_ref[...], axis=0, keepdims=True)
    rz_old, curv_sum, cross, square = (totals[:, place : place + 1] for place in range(4))
    size = rz_old / curv_sum
    ratio = (rz_old - 2.0 * size * cross + size * size * square) / rz_old
    size = jnp.broadcast_to(size, (ROWS, PB))
    ratio = jnp.broadcast_to(ratio, (ROWS, PB))

    chunk = new_solution_ref.shape[1]
    start = pl.program_id(0) * chunk

    def body(index, carry):
        rows = pl.ds(pl.multiple_of(start + index * ROWS, ROWS), ROWS)
        here = pl.ds(pl.multiple_of(index * ROWS, ROWS), ROWS)
        line = [direction_ref[k, rows, :] for k in range(3)]
        new = [residual_ref[k, rows, :] - size * operated_ref[k, rows, :] for k in range(3)]
        applied = precondition([pre_ref[entry, rows, :] for entry in range(6)], new)
        for k in range(3):
            new_solution_ref[k, here, :] = solution_ref[k, rows, :] + size * line[k]
            new_residual_ref[k, here, :] = new[k]
            new_direction_ref[k, here, :] = applied[k] + ratio * line[k]
        return carry

    lax.fori_loop(0, chunk // ROWS, body, 0, unroll=4)


def update_maps(parts, solution, residual, direction, operated, preconditioner, chunk):
    maps = pl.BlockSpec((3, chunk, PB), lambda i: (0, i, 0))
    return pl.pallas_call(
        update_kernel,
        grid=(solution.shape[1] // chunk,),
        out_shape=(jax.ShapeDtypeStruct(solution.shape, F32),) * 3,
        in_specs=[vmem_spec()] * 6,
        out_specs=(maps,) * 3,
        compiler_params=params(16),
        name="update_maps",
    )(parts, solution, residual, direction, operated, preconditioner)


def exchanged(value, axis, bit):
    count = lax.axis_size(axis)
    return lax.ppermute(value, axis, [(source, source ^ bit) for source in range(count)])


def delivered(own, other, sign):
    times, dets = lax.axis_size("tm"), lax.axis_size("det")
    got = exchanged(other, "det", 1)
    pieces = []
    for reach in range(own.shape[0]):
        for hop in range(own.shape[1]):
            pair = jnp.stack([own[reach, hop], got[reach, hop]])
            if reach or hop:
                pair = lax.ppermute(
                    pair,
                    ("tm", "det"),
                    [
                        (time * dets + det, (time + sign * reach) % times * dets + (det ^ (2 * hop)))
                        for time in range(times)
                        for det in range(dets)
                    ],
                )
            pieces.append(pair)
    return pieces


def summed_over_det(value, beside):
    count = lax.axis_size("det")
    half = value.shape[1] // 2
    core = lax.axis_index("det") % 2
    own = lax.dynamic_slice_in_dim(value, core * half, half, 1)
    other = lax.dynamic_slice_in_dim(value, (1 - core) * half, half, 1)
    own = own + exchanged(other, "det", 1)
    bit = 2
    while bit < count:
        own = own + exchanged(own, "det", bit)
        bit *= 2
    own, beside = lax.optimization_barrier((own, beside))
    other = exchanged(own, "det", 1)
    lower = jnp.where(core == 0, own, other)
    upper = jnp.where(core == 0, other, own)
    return jnp.concatenate([lower, upper], axis=1), beside


def on_device(
    solution,
    residual,
    direction,
    preconditioner,
    pull_index,
    block_slot,
    pixel_offset,
    angle_index,
    det_weight,
    mode_templates,
    mode_precision,
):
    det_dev = pixel_offset.shape[0]
    device_count = lax.axis_size("tm") * lax.axis_size("det")
    det = lax.axis_index("det").astype(jnp.int32)[None]
    templates = mode_templates.T
    weight = det_weight[None, :]

    own, other = pull_blocks(det, pull_index, direction)
    pieces = delivered(own, other, -1)
    timeline, local_proj = make_timeline(
        det, block_slot, templates, weight, pixel_offset, angle_index, pieces, 4096
    )
    matrices = mode_matrices(det, det_dev, templates, weight, mode_precision, local_proj)
    projection, (back, own_weight) = summed_over_det(local_proj, matrices)
    own, other = bin_samples(
        det, block_slot, projection, back, own_weight, pixel_offset, angle_index, timeline,
        pull_index.shape[2:], 2048,
    )
    arrived = delivered(own, other, 1)
    operated, parts = push_blocks(
        det, pull_index, direction, residual, preconditioner, arrived, device_count
    )
    parts = lax.all_to_all(parts, ("tm", "det"), split_axis=0, concat_axis=0, tiled=True)
    return update_maps(parts, solution, residual, direction, operated, preconditioner, 192)


def solution(mesh):
    maps = P(None, ("tm", "det"), None)
    samples = P("det", "tm")
    in_specs = (maps,) * 4 + (P("tm", "det", None, None, None),) + (samples,) * 3 + (P(),) * 3
    return jax.shard_map(
        on_device, mesh=mesh, in_specs=in_specs, out_specs=(maps,) * 3, check_vma=False
    )
```

```python
import functools
import math

import jax
import jax.numpy as jnp
import numpy as np
from jax import lax
from jax.experimental import pallas as pl
from jax.experimental.pallas import tpu as pltpu
from jax.sharding import PartitionSpec as P

PB = 128
SB = 128
RUN = 4
NANG = 64
GROUP = 8
RUN_LEN = RUN * SB
ROWS = 8
LOW = 32
HIGH = PB // LOW
F32 = jnp.float32
BF16 = jnp.bfloat16
HIGHEST = lax.Precision.HIGHEST
MIB = 1024 * 1024
COST = 8192
TERMS = 8


def vmem_spec():
    return pl.BlockSpec(memory_space=pltpu.VMEM)


def smem_spec():
    return pl.BlockSpec(memory_space=pltpu.SMEM)


def in_hbm(*arrays):
    return tuple(pltpu.with_memory_space_constraint(array, pltpu.HBM) for array in arrays)


def cost(flops):
    return pl.CostEstimate(flops=flops, bytes_accessed=4 * MIB, transcendentals=0)


def params(mib):
    return pltpu.CompilerParams(vmem_limit_bytes=mib * MIB)


def wave_terms():
    turn = (np.arange(NANG) - NANG // 2).astype(np.float64) / NANG
    powers = np.stack([turn ** (2 * term) for term in range(TERMS)], axis=1)
    even = np.linalg.lstsq(powers, -np.cos(2.0 * math.pi * turn), rcond=None)[0]
    odd = np.linalg.lstsq(powers * turn[:, None], -np.sin(2.0 * math.pi * turn), rcond=None)[0]
    return [float(term) for term in even], [float(term) for term in odd]


EVEN_TERMS, ODD_TERMS = wave_terms()


def waves(angle):
    turn = (angle - NANG // 2).astype(F32) * (1.0 / NANG)
    square = turn * turn
    even = jnp.full_like(turn, EVEN_TERMS[-1])
    odd = jnp.full_like(turn, ODD_TERMS[-1])
    for term in range(TERMS - 2, -1, -1):
        even = even * square + EVEN_TERMS[term]
        odd = odd * square + ODD_TERMS[term]
    return even, odd * turn


def trig_table():
    lane = lax.broadcasted_iota(jnp.int32, (GROUP, PB), 1)
    cos_vals, sin_vals = waves(lane & (NANG - 1))
    return jnp.where(lane < NANG, cos_vals, sin_vals)


def halves(value):
    first = value.astype(BF16)
    rest = value - first.astype(F32)
    second = rest.astype(BF16)
    return first, second, (rest - second.astype(F32)).astype(BF16)


def lane_pick(table, index):
    return jnp.take_along_axis(table, index, axis=1, mode="promise_in_bounds")


def wide_pick(table, index):
    parts = [
        lane_pick(table, index[:, PB * part : PB * (part + 1)])
        for part in range(index.shape[1] // PB)
    ]
    return jnp.concatenate(parts, axis=1)


def precondition(pre, field):
    return (
        pre[0] * field[0] + pre[3] * field[1] + pre[4] * field[2],
        pre[3] * field[0] + pre[1] * field[1] + pre[5] * field[2],
        pre[4] * field[0] + pre[5] * field[1] + pre[2] * field[2],
    )


def partner(det, hop, flip):
    return det ^ (2 * hop + flip)


def pull_kernel(det_ref, request_ref, direction_ref, own_ref, other_ref):
    _, _, reach_count, group_count, cap_count = request_ref.shape
    det = det_ref[0]
    for flip, ref in ((1, other_ref), (0, own_ref)):
        for reach in range(reach_count):
            for hop in range(group_count // 2):
                group = partner(det, hop, flip)
                for slot in range(cap_count):
                    block = request_ref[0, 0, reach, group, slot]
                    for k in range(3):
                        ref[reach, hop, pl.ds(k * cap_count + slot, 1), :] = direction_ref[
                            k, pl.ds(block, 1), :
                        ]


def pull_blocks(det, pull_index, direction):
    _, _, reach_count, group_count, cap_count = pull_index.shape
    piece = jax.ShapeDtypeStruct((reach_count, group_count // 2, 3 * cap_count, PB), F32)
    return pl.pallas_call(
        pull_kernel,
        out_shape=(piece, piece),
        in_specs=[smem_spec(), smem_spec(), vmem_spec()],
        out_specs=(vmem_spec(), vmem_spec()),
        compiler_params=params(24),
        name="pull_blocks",
    )(det, *in_hbm(pull_index, direction))


def own_lanes(ref, first, count):
    rows, total = ref.shape
    value = jnp.broadcast_to(ref[...], (max(rows, ROWS), total))
    return pltpu.roll(value, lax.rem(total - first, total), 1)[:, :count]


def mode_kernel(det_ref, template_ref, weight_ref, precision_ref, after_ref, back_ref, own_weight_ref):
    del after_ref
    det_dev = back_ref.shape[0]
    modes = template_ref.shape[0]
    templates = template_ref[...]
    first = det_ref[0] * det_dev
    own_templates = own_lanes(template_ref, first, det_dev)
    own_weight_ref[...] = own_lanes(weight_ref, first, det_dev).T[:, :1]
    row = lax.broadcasted_iota(jnp.int32, (modes, modes), 0)
    column = lax.broadcasted_iota(jnp.int32, (modes, modes), 1)
    unit = (row == column).astype(F32)
    core = unit * precision_ref[...] + lax.dot_general(
        templates * weight_ref[:1, :], templates, (((1,), (1,)), ((), ())), precision=HIGHEST, preferred_element_type=F32
    )
    inverse = unit
    line = lax.broadcasted_iota(jnp.int32, (modes, 1), 0)
    for step in range(modes):
        root = 1.0 / jnp.sqrt(core[step : step + 1, step : step + 1])
        factor = jnp.where(line > step, core[:, step : step + 1] * root, 0.0)
        core_row = core[step : step + 1, :] * root
        inverse_row = inverse[step : step + 1, :] * root
        core = core - factor * core_row
        inverse = jnp.where(line == step, inverse_row, inverse - factor * inverse_row)
    solved = lax.dot_general(
        inverse, inverse, (((0,), (0,)), ((), ())), precision=HIGHEST, preferred_element_type=F32
    )
    back_ref[...] = jnp.dot(solved, own_templates, precision=HIGHEST, preferred_element_type=F32).T


def mode_matrices(det, det_dev, templates, weight, mode_precision, waited):
    modes = templates.shape[0]
    return pl.pallas_call(
        mode_kernel,
        out_shape=(
            jax.ShapeDtypeStruct((det_dev, modes), F32),
            jax.ShapeDtypeStruct((det_dev, 1), F32),
        ),
        in_specs=[smem_spec(), vmem_spec(), vmem_spec(), vmem_spec(), pl.BlockSpec(memory_space=pl.ANY)],
        out_specs=(vmem_spec(), vmem_spec()),
        compiler_params=params(8),
        name="mode_matrices",
    )(det, *in_hbm(templates, weight, mode_precision[None, :]), waited)


def timeline_kernel(first_step, det_ref, slot_ref, template_ref, weight_ref, offset_ref, angle_ref, *refs):
    *piece_refs, time_ref, proj_ref, map_ref, table_ref, weighted_ref = refs
    step = pl.program_id(0)
    cap_count = piece_refs[0].shape[1] // 3
    hop_count = len(piece_refs) // 2
    det_count, chunk = offset_ref.shape
    runs = chunk // RUN_LEN

    @pl.when(step == 0)
    def _():
        det = det_ref[0]
        first = det * det_count
        weighted_ref[...] = own_lanes(template_ref, first, det_count) * own_lanes(weight_ref, first, det_count)[:1, :]
        for place, ref in enumerate(piece_refs):
            reach, hop = place // hop_count, place % hop_count
            for flip in range(2):
                block = (reach * 2 * hop_count + partner(det, hop, flip)) * cap_count
                first = pl.multiple_of(block * ROWS, cap_count * ROWS)
                for k in range(3):
                    map_ref[pl.ds(first + k, cap_count, stride=ROWS), :] = ref[
                        flip, pl.ds(k * cap_count, cap_count), :
                    ]

    def body(group, carry):
        first = pl.multiple_of(group * GROUP, GROUP)
        for run in range(runs):
            for det in range(GROUP):
                slot = slot_ref[first + det, ((first_step + step) * runs + run) * RUN]
                table_ref[run, pl.ds(det * ROWS, ROWS), :] = map_ref[
                    pl.ds(pl.multiple_of(slot * ROWS, ROWS), ROWS), :
                ]
            tables = [table_ref[run, pl.ds(k, GROUP, stride=ROWS), :] for k in range(3)]
            for part in range(RUN):
                lanes = pl.ds(run * RUN_LEN + part * SB, SB)
                offset = offset_ref[pl.ds(first, GROUP), lanes]
                angle = angle_ref[pl.ds(first, GROUP), lanes]
                cos_vals, sin_vals = waves(angle)
                time_ref[pl.ds(first, GROUP), lanes] = (
                    lane_pick(tables[0], offset)
                    + cos_vals * lane_pick(tables[1], offset)
                    + sin_vals * lane_pick(tables[2], offset)
                )
        return carry

    lax.fori_loop(0, det_count // GROUP, body, 0, unroll=8)
    proj_ref[...] = jnp.dot(
        weighted_ref[...], time_ref[...], precision=HIGHEST, preferred_element_type=F32
    )


def make_timeline(det, block_slot, templates, weight, pixel_offset, angle_index, pieces, chunk, part, parts):
    det_dev, samp_dev = pixel_offset.shape
    steps = samp_dev // parts // chunk
    first_step = part * steps
    modes = templates.shape[0]
    slot_total = len(pieces) * 2 * (pieces[0].shape[1] // 3)
    runs = chunk // RUN_LEN
    wide = pl.BlockSpec((det_dev, chunk), lambda i: (0, first_step + i))
    return pl.pallas_call(
        functools.partial(timeline_kernel, first_step),
        grid=(steps,),
        out_shape=(
            pltpu.HBM((det_dev, steps * chunk), F32),
            jax.ShapeDtypeStruct((modes, steps * chunk), F32),
        ),
        in_specs=[smem_spec(), smem_spec(), vmem_spec(), vmem_spec(), wide, wide] + [vmem_spec()] * len(pieces),
        out_specs=(
            pl.BlockSpec((det_dev, chunk), lambda i: (0, i)),
            pl.BlockSpec((modes, chunk), lambda i: (0, i)),
        ),
        scratch_shapes=[
            pltpu.VMEM((slot_total * ROWS, PB), F32),
            pltpu.VMEM((runs, GROUP * ROWS, PB), F32),
            pltpu.VMEM((modes, det_dev), F32),
        ],
        compiler_params=params(24),
        cost_estimate=cost(det_dev * steps * chunk * COST),
        name="make_timeline",
    )(det, *in_hbm(block_slot, templates, weight, pixel_offset, angle_index), *pieces)


def bin_kernel(
    first_step, shape, begins, ends, det_ref, slot_ref, proj_ref, back_ref, weight_ref, offset_ref, angle_ref, time_ref, *refs
):
    *refs, row_ref, filt_ref = refs
    begin_ref = None if begins else refs.pop(0)
    if ends:
        own_ref, other_ref, map_ref = refs
    else:
        (map_ref,) = refs
    step = pl.program_id(0)
    reach_count, group_count, cap_count = shape
    hop_count = group_count // 2
    det_count, chunk = offset_ref.shape
    runs = chunk // RUN_LEN

    @pl.when(step == 0)
    def _():
        map_ref[...] = jnp.zeros_like(map_ref) if begins else begin_ref[...]
        row_ref[...] = jnp.zeros_like(row_ref)

    back = halves(back_ref[...])
    proj = halves(proj_ref[...])
    orders = ((0, 0), (0, 1), (1, 0), (0, 2), (1, 1), (2, 0))
    common = jnp.dot(
        jnp.concatenate([back[left] for left, _ in orders], axis=1),
        jnp.concatenate([proj[right] for _, right in orders], axis=0),
        preferred_element_type=F32,
    )
    filt_ref[...] = weight_ref[...] * (time_ref[...] - common)
    trig = trig_table()
    det_iota = lax.broadcasted_iota(jnp.int32, (GROUP, RUN_LEN), 0)
    low_iota = lax.broadcasted_iota(jnp.int32, (LOW, RUN_LEN), 0).astype(F32).astype(BF16)
    row_iota = lax.broadcasted_iota(jnp.int32, (GROUP, PB), 0)
    lane_iota = lax.broadcasted_iota(jnp.int32, (GROUP, PB), 1)
    places = [((lane_iota // LOW) - row_iota - j) % HIGH == 0 for j in range(HIGH)]
    zero = jnp.zeros((), BF16)
    one = jnp.ones((), BF16)

    def body(group, carry):
        first = pl.multiple_of(group * GROUP, GROUP)
        for run in range(runs):
            lanes = pl.ds(run * RUN_LEN, RUN_LEN)
            offset = offset_ref[pl.ds(first, GROUP), lanes]
            angle = angle_ref[pl.ds(first, GROUP), lanes]
            filtered = filt_ref[pl.ds(first, GROUP), lanes]
            cos_vals = wide_pick(trig, angle)
            sin_vals = wide_pick(trig, angle + NANG)
            packed = []
            for value in (filtered, cos_vals * filtered, sin_vals * filtered):
                upper = value.astype(BF16).astype(F32)
                packed.append(jnp.concatenate([upper, value - upper], axis=0).astype(BF16))
            turn = ((offset // LOW) - det_iota) & (HIGH - 1)
            turn = turn.astype(F32)
            turn = jnp.concatenate([turn, turn], axis=0).astype(BF16)
            left = jnp.concatenate(
                [jnp.where(turn == jnp.asarray(j, BF16), value, zero) for j in range(HIGH) for value in packed],
                axis=0,
            )
            low = (offset & (LOW - 1)).astype(F32)
            hots = []
            for det in range(GROUP):
                line = jnp.broadcast_to(low[det : det + 1, :], (LOW, RUN_LEN)).astype(BF16)
                hots.append(jnp.where(line == low_iota, one, zero))
            right = jnp.concatenate(hots, axis=0)
            product = lax.dot_general(
                left, right, (((1,), (1,)), ((), ())), preferred_element_type=F32
            )
            for k in range(3):
                total = None
                for j in range(HIGH):
                    top = (j * 3 + k) * 2 * GROUP
                    pair = product[top : top + GROUP] + product[top + GROUP : top + 2 * GROUP]
                    part = jnp.where(row_iota < HIGH, pair[:, :PB], pair[:, PB:])
                    if j:
                        part = pltpu.roll(part, LOW * j, 1)
                    total = part if total is None else jnp.where(places[j], part, total)
                row_ref[run, pl.ds(k, GROUP, stride=ROWS), :] = total
            for det in range(GROUP):
                slot = slot_ref[first + det, ((first_step + step) * runs + run) * RUN]
                at = pl.ds(pl.multiple_of(slot * ROWS, ROWS), ROWS)
                map_ref[at, :] += row_ref[run, pl.ds(det * ROWS, ROWS), :]
        return carry

    lax.fori_loop(0, det_count // GROUP, body, 0, unroll=8)

    if not ends:
        return

    @pl.when(step == pl.num_programs(0) - 1)
    def _():
        det = det_ref[0]
        for flip, ref in ((1, other_ref), (0, own_ref)):
            for reach in range(reach_count):
                for hop in range(hop_count):
                    block = (reach * 2 * hop_count + partner(det, hop, flip)) * cap_count
                    start = pl.multiple_of(block * ROWS, cap_count * ROWS)
                    for k in range(3):
                        ref[reach, hop, pl.ds(k * cap_count, cap_count), :] = map_ref[
                            pl.ds(start + k, cap_count, stride=ROWS), :
                        ]


def bin_samples(
    det, block_slot, projection, back, weight, pixel_offset, angle_index, timeline, shape, chunk, part, parts, begin
):
    det_dev, samp_dev = pixel_offset.shape
    modes = projection.shape[0]
    reach_count, group_count, cap_count = shape
    slot_total = reach_count * group_count * cap_count
    runs = chunk // RUN_LEN
    steps = samp_dev // parts // chunk
    first_step = part * steps
    begins, ends = part == 0, part == parts - 1
    wide = pl.BlockSpec((det_dev, chunk), lambda i: (0, first_step + i))
    piece = jax.ShapeDtypeStruct((reach_count, group_count // 2, 3 * cap_count, PB), F32)
    sums = (slot_total * ROWS, PB)
    return pl.pallas_call(
        functools.partial(bin_kernel, first_step, shape, begins, ends),
        grid=(steps,),
        out_shape=(piece, piece) if ends else jax.ShapeDtypeStruct(sums, F32),
        in_specs=[smem_spec(), smem_spec(), pl.BlockSpec((modes, chunk), lambda i: (0, i))]
        + [vmem_spec()] * 2
        + [wide, wide, pl.BlockSpec((det_dev, chunk), lambda i: (0, i))]
        + ([] if begins else [vmem_spec()]),
        out_specs=(vmem_spec(), vmem_spec()) if ends else vmem_spec(),
        scratch_shapes=([pltpu.VMEM(sums, F32)] if ends else [])
        + [
            pltpu.VMEM((runs, GROUP * ROWS, PB), F32),
            pltpu.VMEM((det_dev, chunk), F32),
        ],
        compiler_params=params(24),
        cost_estimate=cost(2 * det_dev * steps * chunk * COST),
        name="bin_samples",
    )(
        det, *in_hbm(block_slot), projection, back, weight, *in_hbm(pixel_offset, angle_index, timeline),
        *(() if begins else (begin,)),
    )


def push_kernel(det_ref, request_ref, direction_ref, residual_ref, pre_ref, *refs):
    *piece_refs, operated_ref, part_ref = refs
    cap_count = request_ref.shape[4]
    hop_count = len(piece_refs) // 2
    det = det_ref[0]
    operated_ref[...] = jnp.zeros_like(operated_ref)
    for place, ref in enumerate(piece_refs):
        reach, hop = place // hop_count, place % hop_count
        for flip in range(2):
            group = partner(det, hop, flip)
            sums = []
            for slot in range(cap_count):
                block = request_ref[0, 0, reach, group, slot]
                for k in range(3):
                    line = operated_ref[k, pl.ds(block, 1), :]
                    sums.append((block, k, line + ref[flip, pl.ds(k * cap_count + slot, 1), :]))
            for block, k, line in sums:
                operated_ref[k, pl.ds(block, 1), :] = line

    blocks = operated_ref.shape[1]

    def body(index, totals):
        rows = pl.ds(pl.multiple_of(index * ROWS, ROWS), ROWS)
        pre = [pre_ref[entry, rows, :] for entry in range(6)]
        old = [residual_ref[k, rows, :] for k in range(3)]
        oper = [operated_ref[k, rows, :] for k in range(3)]
        line = [direction_ref[k, rows, :] for k in range(3)]
        old_applied = precondition(pre, old)
        oper_applied = precondition(pre, oper)

        def dot(left, right):
            return left[0] * right[0] + left[1] * right[1] + left[2] * right[2]

        parts = (dot(old, old_applied), dot(line, oper), dot(oper, old_applied), dot(oper, oper_applied))
        return tuple(total + part for total, part in zip(totals, parts))

    nothing = jnp.zeros((ROWS, PB), F32)
    totals = lax.fori_loop(0, blocks // ROWS, body, (nothing,) * 4, unroll=8)
    lane = lax.broadcasted_iota(jnp.int32, part_ref.shape, 1)
    row = jnp.zeros(part_ref.shape, F32)
    for place, total in enumerate(totals):
        value = jnp.sum(jnp.sum(total, axis=0, keepdims=True), axis=1, keepdims=True)
        row = jnp.where(lane == place, value, row)
    part_ref[...] = row


def push_blocks(det, pull_index, direction, residual, preconditioner, pieces, device_count):
    return pl.pallas_call(
        push_kernel,
        out_shape=(
            jax.ShapeDtypeStruct(direction.shape, F32),
            jax.ShapeDtypeStruct((device_count, PB), F32),
        ),
        in_specs=[smem_spec(), smem_spec()] + [vmem_spec()] * (3 + len(pieces)),
        out_specs=(vmem_spec(), vmem_spec()),
        compiler_params=params(16),
        name="push_blocks",
    )(det, pull_index, direction, residual, preconditioner, *pieces)


def update_kernel(
    part_ref, solution_ref, residual_ref, direction_ref, operated_ref, pre_ref, new_solution_ref, new_residual_ref, new_direction_ref
):
    totals = jnp.sum(part_ref[...], axis=0, keepdims=True)
    rz_old, curv_sum, cross, square = (totals[:, place : place + 1] for place in range(4))
    size = rz_old / curv_sum
    ratio = (rz_old - 2.0 * size * cross + size * size * square) / rz_old
    size = jnp.broadcast_to(size, (ROWS, PB))
    ratio = jnp.broadcast_to(ratio, (ROWS, PB))

    chunk = new_solution_ref.shape[1]
    start = pl.program_id(0) * chunk

    def body(index, carry):
        rows = pl.ds(pl.multiple_of(start + index * ROWS, ROWS), ROWS)
        here = pl.ds(pl.multiple_of(index * ROWS, ROWS), ROWS)
        line = [direction_ref[k, rows, :] for k in range(3)]
        new = [residual_ref[k, rows, :] - size * operated_ref[k, rows, :] for k in range(3)]
        applied = precondition([pre_ref[entry, rows, :] for entry in range(6)], new)
        for k in range(3):
            new_solution_ref[k, here, :] = solution_ref[k, rows, :] + size * line[k]
            new_residual_ref[k, here, :] = new[k]
            new_direction_ref[k, here, :] = applied[k] + ratio * line[k]
        return carry

    lax.fori_loop(0, chunk // ROWS, body, 0, unroll=4)


def update_maps(parts, solution, residual, direction, operated, preconditioner, chunk):
    maps = pl.BlockSpec((3, chunk, PB), lambda i: (0, i, 0))
    return pl.pallas_call(
        update_kernel,
        grid=(solution.shape[1] // chunk,),
        out_shape=(jax.ShapeDtypeStruct(solution.shape, F32),) * 3,
        in_specs=[vmem_spec()] * 6,
        out_specs=(maps,) * 3,
        compiler_params=params(16),
        name="update_maps",
    )(parts, solution, residual, direction, operated, preconditioner)


def exchanged(value, axis, bit):
    count = lax.axis_size(axis)
    return lax.ppermute(value, axis, [(source, source ^ bit) for source in range(count)])


def delivered(own, other, sign):
    times, dets = lax.axis_size("tm"), lax.axis_size("det")
    got = exchanged(other, "det", 1)
    pieces = []
    for reach in range(own.shape[0]):
        for hop in range(own.shape[1]):
            pair = jnp.stack([own[reach, hop], got[reach, hop]])
            if reach or hop:
                pair = lax.ppermute(
                    pair,
                    ("tm", "det"),
                    [
                        (time * dets + det, (time + sign * reach) % times * dets + (det ^ (2 * hop)))
                        for time in range(times)
                        for det in range(dets)
                    ],
                )
            pieces.append(pair)
    return pieces


def core_sum(value):
    half = value.shape[1] // 2
    core = lax.axis_index("det") % 2
    own = lax.dynamic_slice_in_dim(value, core * half, half, 1)
    other = lax.dynamic_slice_in_dim(value, (1 - core) * half, half, 1)
    return own + exchanged(other, "det", 1)


def x_sum(own):
    bit = 2
    while bit < lax.axis_size("det"):
        own = own + exchanged(own, "det", bit)
        bit *= 2
    return own


def both_halves(own):
    core = lax.axis_index("det") % 2
    other = exchanged(own, "det", 1)
    lower = jnp.where(core == 0, own, other)
    upper = jnp.where(core == 0, other, own)
    return jnp.concatenate([lower, upper], axis=1)


def after(value, *others):
    return lax.optimization_barrier((value, *others))[0]


def on_device(
    solution,
    residual,
    direction,
    preconditioner,
    pull_index,
    block_slot,
    pixel_offset,
    angle_index,
    det_weight,
    mode_templates,
    mode_precision,
):
    det_dev = pixel_offset.shape[0]
    device_count = lax.axis_size("tm") * lax.axis_size("det")
    det = lax.axis_index("det").astype(jnp.int32)[None]
    templates = mode_templates.T
    weight = det_weight[None, :]

    own, other = pull_blocks(det, pull_index, direction)
    pieces = delivered(own, other, -1)
    back, own_weight = mode_matrices(det, det_dev, templates, weight, mode_precision, pieces[1])
    times, projections = [], []
    ready = (back,)
    for part in range(2):
        timeline, local_proj = make_timeline(
            det, block_slot, after(templates, *ready), weight, pixel_offset, angle_index, pieces, 2048, part, 2
        )
        half = core_sum(local_proj)
        ready = (half,)
        times.append(timeline)
        projections.append((x_sum(half), half, local_proj))
    first = both_halves(after(projections[0][0], projections[1][2]))
    sums = bin_samples(
        det, block_slot, after(first, projections[1][1]), back, own_weight, pixel_offset, angle_index, times[0],
        pull_index.shape[2:], 2048, 0, 2, None,
    )
    second = both_halves(after(projections[1][0], sums))
    own, other = bin_samples(
        det, block_slot, second, back, own_weight, pixel_offset, angle_index, times[1],
        pull_index.shape[2:], 2048, 1, 2, sums,
    )
    arrived = delivered(own, other, 1)
    operated, parts = push_blocks(
        det, pull_index, direction, residual, preconditioner, arrived, device_count
    )
    parts = lax.all_to_all(parts, ("tm", "det"), split_axis=0, concat_axis=0, tiled=True)
    return update_maps(parts, solution, residual, direction, operated, preconditioner, 192)


def solution(mesh):
    maps = P(None, ("tm", "det"), None)
    samples = P("det", "tm")
    in_specs = (maps,) * 4 + (P("tm", "det", None, None, None),) + (samples,) * 3 + (P(),) * 3
    return jax.shard_map(
        on_device, mesh=mesh, in_specs=in_specs, out_specs=(maps,) * 3, check_vma=False
    )
```

```python
import functools
import math

import jax
import jax.numpy as jnp
import numpy as np
from jax import lax
from jax.experimental import pallas as pl
from jax.experimental.pallas import tpu as pltpu
from jax.sharding import PartitionSpec as P

PB = 128
SB = 128
RUN = 4
NANG = 64
GROUP = 8
RUN_LEN = RUN * SB
ROWS = 8
LOW = 32
HIGH = PB // LOW
F32 = jnp.float32
BF16 = jnp.bfloat16
HIGHEST = lax.Precision.HIGHEST
MIB = 1024 * 1024
COST = 8192
TERMS = 8


def vmem_spec():
    return pl.BlockSpec(memory_space=pltpu.VMEM)


def smem_spec():
    return pl.BlockSpec(memory_space=pltpu.SMEM)


def in_hbm(*arrays):
    return tuple(pltpu.with_memory_space_constraint(array, pltpu.HBM) for array in arrays)


def cost(flops):
    return pl.CostEstimate(flops=flops, bytes_accessed=4 * MIB, transcendentals=0)


def params(mib):
    return pltpu.CompilerParams(vmem_limit_bytes=mib * MIB)


def wave_terms():
    turn = (np.arange(NANG) - NANG // 2).astype(np.float64) / NANG
    powers = np.stack([turn ** (2 * term) for term in range(TERMS)], axis=1)
    even = np.linalg.lstsq(powers, -np.cos(2.0 * math.pi * turn), rcond=None)[0]
    odd = np.linalg.lstsq(powers * turn[:, None], -np.sin(2.0 * math.pi * turn), rcond=None)[0]
    return [float(term) for term in even], [float(term) for term in odd]


EVEN_TERMS, ODD_TERMS = wave_terms()


def waves(angle):
    turn = (angle - NANG // 2).astype(F32) * (1.0 / NANG)
    square = turn * turn
    even = jnp.full_like(turn, EVEN_TERMS[-1])
    odd = jnp.full_like(turn, ODD_TERMS[-1])
    for term in range(TERMS - 2, -1, -1):
        even = even * square + EVEN_TERMS[term]
        odd = odd * square + ODD_TERMS[term]
    return even, odd * turn


def trig_table():
    lane = lax.broadcasted_iota(jnp.int32, (GROUP, PB), 1)
    cos_vals, sin_vals = waves(lane & (NANG - 1))
    return jnp.where(lane < NANG, cos_vals, sin_vals)


def halves(value):
    first = value.astype(BF16)
    rest = value - first.astype(F32)
    second = rest.astype(BF16)
    return first, second, (rest - second.astype(F32)).astype(BF16)


def lane_pick(table, index):
    return jnp.take_along_axis(table, index, axis=1, mode="promise_in_bounds")


def wide_pick(table, index):
    parts = [
        lane_pick(table, index[:, PB * part : PB * (part + 1)])
        for part in range(index.shape[1] // PB)
    ]
    return jnp.concatenate(parts, axis=1)


def precondition(pre, field):
    return (
        pre[0] * field[0] + pre[3] * field[1] + pre[4] * field[2],
        pre[3] * field[0] + pre[1] * field[1] + pre[5] * field[2],
        pre[4] * field[0] + pre[5] * field[1] + pre[2] * field[2],
    )


def partner(det, hop, flip):
    return det ^ (2 * hop + flip)


def pull_kernel(det_ref, request_ref, direction_ref, own_ref, other_ref):
    _, _, reach_count, group_count, cap_count = request_ref.shape
    det = det_ref[0]
    for flip, ref in ((1, other_ref), (0, own_ref)):
        for reach in range(reach_count):
            for hop in range(group_count // 2):
                group = partner(det, hop, flip)
                for slot in range(cap_count):
                    block = request_ref[0, 0, reach, group, slot]
                    for k in range(3):
                        ref[reach, hop, pl.ds(k * cap_count + slot, 1), :] = direction_ref[
                            k, pl.ds(block, 1), :
                        ]


def pull_blocks(det, pull_index, direction):
    _, _, reach_count, group_count, cap_count = pull_index.shape
    piece = jax.ShapeDtypeStruct((reach_count, group_count // 2, 3 * cap_count, PB), F32)
    return pl.pallas_call(
        pull_kernel,
        out_shape=(piece, piece),
        in_specs=[smem_spec(), smem_spec(), vmem_spec()],
        out_specs=(vmem_spec(), vmem_spec()),
        compiler_params=params(24),
        name="pull_blocks",
    )(det, *in_hbm(pull_index, direction))


def own_lanes(ref, first, count):
    rows, total = ref.shape
    value = jnp.broadcast_to(ref[...], (max(rows, ROWS), total))
    return pltpu.roll(value, lax.rem(total - first, total), 1)[:, :count]


def mode_kernel(det_ref, template_ref, weight_ref, precision_ref, after_ref, back_ref, own_weight_ref):
    del after_ref
    det_dev = back_ref.shape[0]
    modes = template_ref.shape[0]
    templates = template_ref[...]
    first = det_ref[0] * det_dev
    own_templates = own_lanes(template_ref, first, det_dev)
    own_weight_ref[...] = own_lanes(weight_ref, first, det_dev).T[:, :1]
    row = lax.broadcasted_iota(jnp.int32, (modes, modes), 0)
    column = lax.broadcasted_iota(jnp.int32, (modes, modes), 1)
    unit = (row == column).astype(F32)
    core = unit * precision_ref[...] + lax.dot_general(
        templates * weight_ref[:1, :], templates, (((1,), (1,)), ((), ())), precision=HIGHEST, preferred_element_type=F32
    )
    inverse = unit
    line = lax.broadcasted_iota(jnp.int32, (modes, 1), 0)
    for step in range(modes):
        root = 1.0 / jnp.sqrt(core[step : step + 1, step : step + 1])
        factor = jnp.where(line > step, core[:, step : step + 1] * root, 0.0)
        core_row = core[step : step + 1, :] * root
        inverse_row = inverse[step : step + 1, :] * root
        core = core - factor * core_row
        inverse = jnp.where(line == step, inverse_row, inverse - factor * inverse_row)
    solved = lax.dot_general(
        inverse, inverse, (((0,), (0,)), ((), ())), precision=HIGHEST, preferred_element_type=F32
    )
    back_ref[...] = jnp.dot(solved, own_templates, precision=HIGHEST, preferred_element_type=F32).T


def mode_matrices(det, det_dev, templates, weight, mode_precision, waited):
    modes = templates.shape[0]
    return pl.pallas_call(
        mode_kernel,
        out_shape=(
            jax.ShapeDtypeStruct((det_dev, modes), F32),
            jax.ShapeDtypeStruct((det_dev, 1), F32),
        ),
        in_specs=[smem_spec(), vmem_spec(), vmem_spec(), vmem_spec(), pl.BlockSpec(memory_space=pl.ANY)],
        out_specs=(vmem_spec(), vmem_spec()),
        compiler_params=params(8),
        name="mode_matrices",
    )(det, *in_hbm(templates, weight, mode_precision[None, :]), waited)


def timeline_kernel(first_step, det_ref, slot_ref, template_ref, weight_ref, offset_ref, angle_ref, *refs):
    *piece_refs, time_ref, proj_ref, map_ref, table_ref, weighted_ref = refs
    step = pl.program_id(0)
    cap_count = piece_refs[0].shape[1] // 3
    hop_count = len(piece_refs) // 2
    det_count, chunk = offset_ref.shape
    runs = chunk // RUN_LEN

    @pl.when(step == 0)
    def _():
        det = det_ref[0]
        first = det * det_count
        weighted_ref[...] = own_lanes(template_ref, first, det_count) * own_lanes(weight_ref, first, det_count)[:1, :]
        for place, ref in enumerate(piece_refs):
            reach, hop = place // hop_count, place % hop_count
            for flip in range(2):
                block = (reach * 2 * hop_count + partner(det, hop, flip)) * cap_count
                first = pl.multiple_of(block * ROWS, cap_count * ROWS)
                for k in range(3):
                    map_ref[pl.ds(first + k, cap_count, stride=ROWS), :] = ref[
                        flip, pl.ds(k * cap_count, cap_count), :
                    ]

    def body(group, carry):
        first = pl.multiple_of(group * GROUP, GROUP)
        for run in range(runs):
            for det in range(GROUP):
                slot = slot_ref[first + det, ((first_step + step) * runs + run) * RUN]
                table_ref[run, pl.ds(det * ROWS, ROWS), :] = map_ref[
                    pl.ds(pl.multiple_of(slot * ROWS, ROWS), ROWS), :
                ]
            tables = [table_ref[run, pl.ds(k, GROUP, stride=ROWS), :] for k in range(3)]
            for part in range(RUN):
                lanes = pl.ds(run * RUN_LEN + part * SB, SB)
                offset = offset_ref[pl.ds(first, GROUP), lanes]
                angle = angle_ref[pl.ds(first, GROUP), lanes]
                cos_vals, sin_vals = waves(angle)
                time_ref[pl.ds(first, GROUP), lanes] = (
                    lane_pick(tables[0], offset)
                    + cos_vals * lane_pick(tables[1], offset)
                    + sin_vals * lane_pick(tables[2], offset)
                )
        return carry

    lax.fori_loop(0, det_count // GROUP, body, 0, unroll=8)
    proj_ref[...] = jnp.dot(
        weighted_ref[...], time_ref[...], precision=HIGHEST, preferred_element_type=F32
    )


def make_timeline(det, block_slot, templates, weight, pixel_offset, angle_index, pieces, chunk, part, parts):
    det_dev, samp_dev = pixel_offset.shape
    steps = samp_dev // parts // chunk
    first_step = part * steps
    modes = templates.shape[0]
    slot_total = len(pieces) * 2 * (pieces[0].shape[1] // 3)
    runs = chunk // RUN_LEN
    wide = pl.BlockSpec((det_dev, chunk), lambda i: (0, first_step + i))
    return pl.pallas_call(
        functools.partial(timeline_kernel, first_step),
        grid=(steps,),
        out_shape=(
            pltpu.HBM((det_dev, steps * chunk), F32),
            jax.ShapeDtypeStruct((modes, steps * chunk), F32),
        ),
        in_specs=[smem_spec(), smem_spec(), vmem_spec(), vmem_spec(), wide, wide] + [vmem_spec()] * len(pieces),
        out_specs=(
            pl.BlockSpec((det_dev, chunk), lambda i: (0, i)),
            pl.BlockSpec((modes, chunk), lambda i: (0, i)),
        ),
        scratch_shapes=[
            pltpu.VMEM((slot_total * ROWS, PB), F32),
            pltpu.VMEM((runs, GROUP * ROWS, PB), F32),
            pltpu.VMEM((modes, det_dev), F32),
        ],
        compiler_params=params(24),
        cost_estimate=cost(det_dev * steps * chunk * COST),
        name="make_timeline",
    )(det, *in_hbm(block_slot, templates, weight, pixel_offset, angle_index), *pieces)


def bin_kernel(
    first_step, shape, begins, ends, det_ref, slot_ref, proj_ref, back_ref, weight_ref, offset_ref, angle_ref, time_ref, *refs
):
    *refs, row_ref, filt_ref = refs
    begin_ref = None if begins else refs.pop(0)
    if ends:
        own_ref, other_ref, map_ref = refs
    else:
        (map_ref,) = refs
    step = pl.program_id(0)
    reach_count, group_count, cap_count = shape
    hop_count = group_count // 2
    det_count, chunk = offset_ref.shape
    runs = chunk // RUN_LEN

    @pl.when(step == 0)
    def _():
        map_ref[...] = jnp.zeros_like(map_ref) if begins else begin_ref[...]
        row_ref[...] = jnp.zeros_like(row_ref)

    back = halves(back_ref[...])
    proj = halves(proj_ref[...])
    orders = ((0, 0), (0, 1), (1, 0), (0, 2), (1, 1), (2, 0))
    common = jnp.dot(
        jnp.concatenate([back[left] for left, _ in orders], axis=1),
        jnp.concatenate([proj[right] for _, right in orders], axis=0),
        preferred_element_type=F32,
    )
    filt_ref[...] = weight_ref[...] * (time_ref[...] - common)
    trig = trig_table()
    det_iota = lax.broadcasted_iota(jnp.int32, (GROUP, RUN_LEN), 0)
    low_iota = lax.broadcasted_iota(jnp.int32, (LOW, RUN_LEN), 0).astype(F32).astype(BF16)
    row_iota = lax.broadcasted_iota(jnp.int32, (GROUP, PB), 0)
    lane_iota = lax.broadcasted_iota(jnp.int32, (GROUP, PB), 1)
    places = [((lane_iota // LOW) - row_iota - j) % HIGH == 0 for j in range(HIGH)]
    zero = jnp.zeros((), BF16)
    one = jnp.ones((), BF16)

    def body(group, carry):
        first = pl.multiple_of(group * GROUP, GROUP)
        for run in range(runs):
            lanes = pl.ds(run * RUN_LEN, RUN_LEN)
            offset = offset_ref[pl.ds(first, GROUP), lanes]
            angle = angle_ref[pl.ds(first, GROUP), lanes]
            filtered = filt_ref[pl.ds(first, GROUP), lanes]
            cos_vals = wide_pick(trig, angle)
            sin_vals = wide_pick(trig, angle + NANG)
            packed = []
            for value in (filtered, cos_vals * filtered, sin_vals * filtered):
                upper = value.astype(BF16).astype(F32)
                packed.append(jnp.concatenate([upper, value - upper], axis=0).astype(BF16))
            turn = ((offset // LOW) - det_iota) & (HIGH - 1)
            turn = turn.astype(F32)
            turn = jnp.concatenate([turn, turn], axis=0).astype(BF16)
            left = jnp.concatenate(
                [jnp.where(turn == jnp.asarray(j, BF16), value, zero) for j in range(HIGH) for value in packed],
                axis=0,
            )
            low = (offset & (LOW - 1)).astype(F32)
            hots = []
            for det in range(GROUP):
                line = jnp.broadcast_to(low[det : det + 1, :], (LOW, RUN_LEN)).astype(BF16)
                hots.append(jnp.where(line == low_iota, one, zero))
            right = jnp.concatenate(hots, axis=0)
            product = lax.dot_general(
                left, right, (((1,), (1,)), ((), ())), preferred_element_type=F32
            )
            for k in range(3):
                total = None
                for j in range(HIGH):
                    top = (j * 3 + k) * 2 * GROUP
                    pair = product[top : top + GROUP] + product[top + GROUP : top + 2 * GROUP]
                    part = jnp.where(row_iota < HIGH, pair[:, :PB], pair[:, PB:])
                    if j:
                        part = pltpu.roll(part, LOW * j, 1)
                    total = part if total is None else jnp.where(places[j], part, total)
                row_ref[run, pl.ds(k, GROUP, stride=ROWS), :] = total
            for det in range(GROUP):
                slot = slot_ref[first + det, ((first_step + step) * runs + run) * RUN]
                at = pl.ds(pl.multiple_of(slot * ROWS, ROWS), ROWS)
                map_ref[at, :] += row_ref[run, pl.ds(det * ROWS, ROWS), :]
        return carry

    lax.fori_loop(0, det_count // GROUP, body, 0, unroll=8)

    if not ends:
        return

    @pl.when(step == pl.num_programs(0) - 1)
    def _():
        det = det_ref[0]
        for flip, ref in ((1, other_ref), (0, own_ref)):
            for reach in range(reach_count):
                for hop in range(hop_count):
                    block = (reach * 2 * hop_count + partner(det, hop, flip)) * cap_count
                    start = pl.multiple_of(block * ROWS, cap_count * ROWS)
                    for k in range(3):
                        ref[reach, hop, pl.ds(k * cap_count, cap_count), :] = map_ref[
                            pl.ds(start + k, cap_count, stride=ROWS), :
                        ]


def bin_samples(
    det, block_slot, projection, back, weight, pixel_offset, angle_index, timeline, shape, chunk, part, parts, begin
):
    det_dev, samp_dev = pixel_offset.shape
    modes = projection.shape[0]
    reach_count, group_count, cap_count = shape
    slot_total = reach_count * group_count * cap_count
    runs = chunk // RUN_LEN
    steps = samp_dev // parts // chunk
    first_step = part * steps
    begins, ends = part == 0, part == parts - 1
    wide = pl.BlockSpec((det_dev, chunk), lambda i: (0, first_step + i))
    piece = jax.ShapeDtypeStruct((reach_count, group_count // 2, 3 * cap_count, PB), F32)
    sums = (slot_total * ROWS, PB)
    return pl.pallas_call(
        functools.partial(bin_kernel, first_step, shape, begins, ends),
        grid=(steps,),
        out_shape=(piece, piece) if ends else jax.ShapeDtypeStruct(sums, F32),
        in_specs=[smem_spec(), smem_spec(), pl.BlockSpec((modes, chunk), lambda i: (0, i))]
        + [vmem_spec()] * 2
        + [wide, wide, pl.BlockSpec((det_dev, chunk), lambda i: (0, i))]
        + ([] if begins else [vmem_spec()]),
        out_specs=(vmem_spec(), vmem_spec()) if ends else vmem_spec(),
        scratch_shapes=([pltpu.VMEM(sums, F32)] if ends else [])
        + [
            pltpu.VMEM((runs, GROUP * ROWS, PB), F32),
            pltpu.VMEM((det_dev, chunk), F32),
        ],
        compiler_params=params(24),
        cost_estimate=cost(2 * det_dev * steps * chunk * COST),
        name="bin_samples",
    )(
        det, *in_hbm(block_slot), projection, back, weight, *in_hbm(pixel_offset, angle_index, timeline),
        *(() if begins else (begin,)),
    )


def push_kernel(det_ref, request_ref, direction_ref, residual_ref, pre_ref, *refs):
    *piece_refs, operated_ref, part_ref = refs
    cap_count = request_ref.shape[4]
    hop_count = len(piece_refs) // 2
    det = det_ref[0]
    operated_ref[...] = jnp.zeros_like(operated_ref)
    for place, ref in enumerate(piece_refs):
        reach, hop = place // hop_count, place % hop_count
        for flip in range(2):
            group = partner(det, hop, flip)
            sums = []
            for slot in range(cap_count):
                block = request_ref[0, 0, reach, group, slot]
                for k in range(3):
                    line = operated_ref[k, pl.ds(block, 1), :]
                    sums.append((block, k, line + ref[flip, pl.ds(k * cap_count + slot, 1), :]))
            for block, k, line in sums:
                operated_ref[k, pl.ds(block, 1), :] = line

    blocks = operated_ref.shape[1]

    def body(index, totals):
        rows = pl.ds(pl.multiple_of(index * ROWS, ROWS), ROWS)
        pre = [pre_ref[entry, rows, :] for entry in range(6)]
        old = [residual_ref[k, rows, :] for k in range(3)]
        oper = [operated_ref[k, rows, :] for k in range(3)]
        line = [direction_ref[k, rows, :] for k in range(3)]
        old_applied = precondition(pre, old)
        oper_applied = precondition(pre, oper)

        def dot(left, right):
            return left[0] * right[0] + left[1] * right[1] + left[2] * right[2]

        parts = (dot(old, old_applied), dot(line, oper), dot(oper, old_applied), dot(oper, oper_applied))
        return tuple(total + part for total, part in zip(totals, parts))

    nothing = jnp.zeros((ROWS, PB), F32)
    totals = lax.fori_loop(0, blocks // ROWS, body, (nothing,) * 4, unroll=8)
    lane = lax.broadcasted_iota(jnp.int32, part_ref.shape, 1)
    row = jnp.zeros(part_ref.shape, F32)
    for place, total in enumerate(totals):
        value = jnp.sum(jnp.sum(total, axis=0, keepdims=True), axis=1, keepdims=True)
        row = jnp.where(lane == place, value, row)
    part_ref[...] = row


def push_blocks(det, pull_index, direction, residual, preconditioner, pieces, device_count):
    return pl.pallas_call(
        push_kernel,
        out_shape=(
            jax.ShapeDtypeStruct(direction.shape, F32),
            jax.ShapeDtypeStruct((device_count, PB), F32),
        ),
        in_specs=[smem_spec(), smem_spec()] + [vmem_spec()] * (3 + len(pieces)),
        out_specs=(vmem_spec(), vmem_spec()),
        compiler_params=params(16),
        name="push_blocks",
    )(det, pull_index, direction, residual, preconditioner, *pieces)


def update_kernel(
    part_ref, solution_ref, residual_ref, direction_ref, operated_ref, pre_ref, new_solution_ref, new_residual_ref, new_direction_ref
):
    totals = jnp.sum(part_ref[...], axis=0, keepdims=True)
    rz_old, curv_sum, cross, square = (totals[:, place : place + 1] for place in range(4))
    size = rz_old / curv_sum
    ratio = (rz_old - 2.0 * size * cross + size * size * square) / rz_old
    size = jnp.broadcast_to(size, (ROWS, PB))
    ratio = jnp.broadcast_to(ratio, (ROWS, PB))

    chunk = new_solution_ref.shape[1]
    start = pl.program_id(0) * chunk

    def body(index, carry):
        rows = pl.ds(pl.multiple_of(start + index * ROWS, ROWS), ROWS)
        here = pl.ds(pl.multiple_of(index * ROWS, ROWS), ROWS)
        line = [direction_ref[k, rows, :] for k in range(3)]
        new = [residual_ref[k, rows, :] - size * operated_ref[k, rows, :] for k in range(3)]
        applied = precondition([pre_ref[entry, rows, :] for entry in range(6)], new)
        for k in range(3):
            new_solution_ref[k, here, :] = solution_ref[k, rows, :] + size * line[k]
            new_residual_ref[k, here, :] = new[k]
            new_direction_ref[k, here, :] = applied[k] + ratio * line[k]
        return carry

    lax.fori_loop(0, chunk // ROWS, body, 0, unroll=4)


def update_maps(parts, solution, residual, direction, operated, preconditioner, chunk):
    maps = pl.BlockSpec((3, chunk, PB), lambda i: (0, i, 0))
    return pl.pallas_call(
        update_kernel,
        grid=(solution.shape[1] // chunk,),
        out_shape=(jax.ShapeDtypeStruct(solution.shape, F32),) * 3,
        in_specs=[vmem_spec()] * 6,
        out_specs=(maps,) * 3,
        compiler_params=params(16),
        name="update_maps",
    )(parts, solution, residual, direction, operated, preconditioner)


def exchanged(value, axis, bit):
    count = lax.axis_size(axis)
    return lax.ppermute(value, axis, [(source, source ^ bit) for source in range(count)])


def delivered(own, other, sign):
    times, dets = lax.axis_size("tm"), lax.axis_size("det")
    got = exchanged(other, "det", 1)
    pieces = []
    for reach in range(own.shape[0]):
        for hop in range(own.shape[1]):
            pair = jnp.stack([own[reach, hop], got[reach, hop]])
            if reach or hop:
                pair = lax.ppermute(
                    pair,
                    ("tm", "det"),
                    [
                        (time * dets + det, (time + sign * reach) % times * dets + (det ^ (2 * hop)))
                        for time in range(times)
                        for det in range(dets)
                    ],
                )
            pieces.append(pair)
    return pieces, got


def core_sum(value):
    half = value.shape[1] // 2
    core = lax.axis_index("det") % 2
    own = lax.dynamic_slice_in_dim(value, core * half, half, 1)
    other = lax.dynamic_slice_in_dim(value, (1 - core) * half, half, 1)
    return own + exchanged(other, "det", 1)


def x_sum(own):
    bit = 2
    while bit < lax.axis_size("det"):
        own = own + exchanged(own, "det", bit)
        bit *= 2
    return own


def both_halves(own):
    core = lax.axis_index("det") % 2
    other = exchanged(own, "det", 1)
    lower = jnp.where(core == 0, own, other)
    upper = jnp.where(core == 0, other, own)
    return jnp.concatenate([lower, upper], axis=1)


def after(value, *others):
    return lax.optimization_barrier((value, *others))[0]


def on_device(
    solution,
    residual,
    direction,
    preconditioner,
    pull_index,
    block_slot,
    pixel_offset,
    angle_index,
    det_weight,
    mode_templates,
    mode_precision,
):
    det_dev = pixel_offset.shape[0]
    device_count = lax.axis_size("tm") * lax.axis_size("det")
    det = lax.axis_index("det").astype(jnp.int32)[None]
    templates = mode_templates.T
    weight = det_weight[None, :]

    own, other = pull_blocks(det, pull_index, direction)
    pieces, got = delivered(own, other, -1)
    back, own_weight = mode_matrices(det, det_dev, templates, weight, mode_precision, got)
    times, projections = [], []
    ready = (back,)
    for part in range(2):
        timeline, local_proj = make_timeline(
            det, block_slot, after(templates, *ready), weight, pixel_offset, angle_index, pieces, 2048, part, 2
        )
        half = core_sum(local_proj)
        ready = (half,)
        times.append(timeline)
        projections.append((x_sum(half), half, local_proj))
    first = both_halves(after(projections[0][0], projections[1][2]))
    sums = bin_samples(
        det, block_slot, after(first, projections[1][1]), back, own_weight, pixel_offset, angle_index, times[0],
        pull_index.shape[2:], 2048, 0, 2, None,
    )
    second = both_halves(after(projections[1][0], sums))
    own, other = bin_samples(
        det, block_slot, second, back, own_weight, pixel_offset, angle_index, times[1],
        pull_index.shape[2:], 2048, 1, 2, sums,
    )
    arrived, _ = delivered(own, other, 1)
    operated, parts = push_blocks(
        det, pull_index, direction, residual, preconditioner, arrived, device_count
    )
    parts = lax.all_to_all(parts, ("tm", "det"), split_axis=0, concat_axis=0, tiled=True)
    return update_maps(parts, solution, residual, direction, operated, preconditioner, 192)


def solution(mesh):
    maps = P(None, ("tm", "det"), None)
    samples = P("det", "tm")
    in_specs = (maps,) * 4 + (P("tm", "det", None, None, None),) + (samples,) * 3 + (P(),) * 3
    return jax.shard_map(
        on_device, mesh=mesh, in_specs=in_specs, out_specs=(maps,) * 3, check_vma=False
    )
```
